32 devices in a mesh: lat: 4 (over z), lon: 8 (over y, x, core).
Axes of the slice: x: 2, y: 2, z: 4, core: 2. Of those that a mesh axis runs over, the one named last changes fastest.
Arguments:
- fields: float32 [256, 256, 256], P('lat', 'lon'), may hold values from -6 to 6
- land_sea: int32 [128, 128], P('lat', 'lon'), may hold values 0 or 1
- w_depth: float32 [3, 3, 256], replicated, may hold values from -2 to 2
- b_depth: float32 [256], replicated, may hold values from -3 to 3
- w_one: bfloat16 [3, 3, 256, 300], replicated, may hold values from -0.125 to 0.125
- b_one: float32 [300], replicated, may hold values from -3 to 3
- w_two: bfloat16 [3, 3, 300, 300], replicated, may hold values from -0.125 to 0.125
- b_two: float32 [300], replicated, may hold values from -3 to 3
Outputs:
- level_out: float32 [128, 128, 300], P('lat', 'lon')
The draws below stay inside these ranges and needn't reach their ends.
All inputs are finite; a program needn't handle non-finite values. No bound on the sum of `land_sea` on one device may be relied on, other than what follows from the above.
Results may differ from the reference program's by a relative error of at most 0.0035.
Values may be sent and summed in bfloat16 or wider, within the bound.
A program may use at most 64 MiB of HBM per device.

```python
import jax
import jax.numpy as jnp
from jax import lax

IN_CH = 256
OUT_CH = 300
LAT_CELLS = 128
LON_CELLS = 128
HALF_LAT = 256
HALF_LON = 256


def place_ends(drawn, own_key, least, largest):
    place = [jax.random.randint(jax.random.fold_in(own_key, axis), (), 0, length) for axis, length in enumerate(drawn.shape)]
    widest = drawn.shape.index(max(drawn.shape))
    beside = place[:widest] + [(place[widest] + 1) % drawn.shape[widest]] + place[widest + 1:]
    return drawn.at[tuple(place)].set(least).at[tuple(beside)].set(largest)


def levels(key, dims, cuts, smallest, largest):
    level, own = 1.0, jax.random.fold_in(key, 6)
    for axis_at, shards_of in cuts:
        heights = jnp.exp(jax.random.uniform(jax.random.fold_in(own, axis_at), (shards_of,), jnp.float32, smallest / len(cuts), largest / len(cuts)))
        level = level * jnp.repeat(heights, dims[axis_at] // shards_of).reshape([-1 if axis == axis_at else 1 for axis in range(len(dims))])
    return level


def scatter_about(rng, shape, scale, bound, split=(), dtype=jnp.bfloat16):
    array = scale * jax.random.normal(rng, shape, jnp.float32)
    if split:
        array = array * levels(rng, shape, split, -0.22, 0.18)
    return jnp.clip(array, -bound, bound).astype(dtype)


def setup_inputs(seed: int = 0) -> dict:
    splits = jax.random.split(jax.random.key(seed), 9)
    fields = scatter_about(splits[0], (HALF_LAT, HALF_LON, IN_CH), 1.0, 6.0, ((0, 4), (1, 8)), jnp.float32)
    land_sea = place_ends((jax.random.randint(splits[1], (LAT_CELLS, LON_CELLS), 0, 10) < 7).astype(jnp.int32), jax.random.fold_in(splits[1], 1), 0, 1)
    w_depth = scatter_about(splits[2], (3, 3, IN_CH), 9 ** -0.5, 2.0, (), jnp.float32)
    b_depth = scatter_about(splits[3], (IN_CH,), 0.5, 3.0, (), jnp.float32)
    w_one = scatter_about(splits[4], (3, 3, IN_CH, OUT_CH), (9 * IN_CH) ** -0.5, 0.125)
    b_one = scatter_about(splits[5], (OUT_CH,), 0.5, 3.0, (), jnp.float32)
    w_two = scatter_about(splits[6], (3, 3, OUT_CH, OUT_CH), (9 * OUT_CH) ** -0.5, 0.125)
    b_two = scatter_about(splits[7], (OUT_CH,), 0.5, 3.0, (), jnp.float32)
    return dict(fields=fields, land_sea=land_sea, w_depth=w_depth, b_depth=b_depth, w_one=w_one, b_one=b_one, w_two=w_two, b_two=b_two)


def cycle_pad(field, reach):
    wide = jnp.concatenate([field[:, -reach:], field, field[:, :reach]], axis=1)
    return jnp.pad(wide, ((reach, reach), (0, 0), (0, 0)))


def dilated(field, kernel, bias, reach):
    rows, cols = field.shape[0], field.shape[1]
    ext = cycle_pad(field, reach).astype(jnp.float32)
    weights = kernel.astype(jnp.float32)
    total = jnp.zeros((rows, cols, kernel.shape[3]), jnp.float32) + bias
    for a in range(3):
        for b in range(3):
            piece = ext[a * reach:a * reach + rows, b * reach:b * reach + cols]
            total = total + jnp.einsum("ijc,cd->ijd", piece, weights[a, b], precision=lax.Precision.HIGHEST)
    return total


def reference(fields, land_sea, w_depth, b_depth, w_one, b_one, w_two, b_two):
    rows = fields.shape[0] // 2
    cols = fields.shape[1] // 2
    wide = jnp.concatenate([fields[:, -1:], fields], axis=1)
    padded = jnp.pad(wide, ((1, 0), (0, 0), (0, 0)))
    down = jnp.zeros((rows, cols, fields.shape[2]), jnp.float32) + b_depth
    for a in range(3):
        for b in range(3):
            down = down + padded[a:a + 2 * rows:2, b:b + 2 * cols:2] * w_depth[a, b]
    mask = land_sea.astype(jnp.float32)[:, :, None]
    down_bf = (down * mask).astype(jnp.bfloat16)
    hidden = jax.nn.gelu(dilated(down_bf, w_one, b_one, 4), approximate=False).astype(jnp.bfloat16)
    return jax.nn.gelu(dilated(hidden, w_two, b_two, 8), approximate=False) * mask
```

```python
import functools

import jax
import jax.numpy as jnp
from jax import lax
from jax.experimental import pallas as pl
from jax.experimental.pallas import tpu as pltpu
from jax.sharding import PartitionSpec as P

MESH = pl.DeviceIdType.MESH
SIDES = tuple((dp, dq) for dp in (-1, 0, 1) for dq in (-1, 0, 1) if (dp, dq) != (0, 0))
STEP = 4
LANES = 128


def gelu(x):
    return 0.5 * x * (1.0 + lax.erf(x * 0.7071067811865476))


def up_to(value, multiple):
    return -(-value // multiple) * multiple


def kernel(
    shape, fields, land, w_depth, b_depth, w_one, b_one, w_two, b_two, out,
    grid, edge, west, corner, mask, down, hidden, one, two, two_tail, result,
    load_sem, edge_sem, down_sem, hidden_sem, out_sem,
):
    n_lat, n_lon, rows, cols, chans, feats = shape
    bands, sectors = rows // STEP, cols // STEP
    main = feats // (2 * LANES) * (2 * LANES)
    tail = feats - main
    lat, lon = lax.axis_index("lat"), lax.axis_index("lon")
    has = {-1: lat > 0, 0: True, 1: lat < n_lat - 1}

    def when(dp, body):
        if dp == 0:
            body()
        else:
            pl.when(has[dp])(body)

    def device(dp, dq):
        return (lat + dp, lax.rem(lon + dq + n_lon, n_lon))

    halves = chans // LANES
    parts = [
        pltpu.make_async_copy(
            fields.at[:, :, h * LANES : (h + 1) * LANES], grid.at[h, 1:, 8:, :], load_sem.at[2 + h])
        for h in range(halves)
    ]
    load_one = pltpu.make_async_copy(w_one, one, load_sem.at[0])
    load_two = pltpu.make_async_copy(w_two, two, load_sem.at[1])
    for load in parts + [load_one, load_two]:
        load.start()

    barrier = pltpu.get_barrier_semaphore()
    for dp, dq in SIDES:
        when(dp, lambda dp=dp, dq=dq: pl.semaphore_signal(
            barrier, inc=1, device_id=device(dp, dq), device_id_type=MESH))

    cells = land[...].astype(jnp.float32)
    eye = lax.broadcasted_iota(jnp.int32, (cols, cols), 0) == lax.broadcasted_iota(
        jnp.int32, (cols, cols), 1)
    for i in range(rows):
        spread = jnp.where(eye, jnp.broadcast_to(cells[i : i + 1], (cols, cols)), 0.0)
        mask[i] = jnp.broadcast_to(jnp.sum(spread, axis=1, keepdims=True), mask.shape[1:])

    if tail:
        hidden[:, :, :, main:] = jnp.zeros(hidden.shape[:3] + (hidden.shape[3] - main,), hidden.dtype)

    def clear(buffer, width):
        gap = jnp.zeros((width,) + buffer.shape[1:], buffer.dtype)

        def north():
            buffer[0:width] = gap

        def south():
            buffer[buffer.shape[0] - width :] = gap

        pl.when(lat == 0)(north)
        pl.when(lat == n_lat - 1)(south)

    clear(down, 1)
    clear(hidden, 2)

    for h in range(halves):
        parts[h].wait()
        for r in range(2 * rows):
            edge[h, r : r + 1, :] = grid[h, 1 + r, 8 + 2 * cols - 1 : 8 + 2 * cols, :]

    pl.semaphore_wait(barrier, 2 + 3 * jnp.minimum(lat, 1) + 3 * jnp.minimum(n_lat - 1 - lat, 1))

    def remote(src, dst, sems, k, dp, dq):
        return pltpu.make_async_remote_copy(
            src_ref=src, dst_ref=dst, send_sem=sems.at[0, k], recv_sem=sems.at[1, k],
            device_id=device(dp, dq), device_id_type=MESH)

    last_row = remote(grid.at[:, 2 * rows, 8:, :], grid.at[:, 0, 8:, :], edge_sem, 0, 1, 0)
    last_col = remote(edge, west, edge_sem, 1, 0, 1)
    last_cell = remote(edge.at[:, 2 * rows - 8 :], corner, edge_sem, 2, 1, 1)
    last_col.start()

    def send_south():
        last_row.start()
        last_cell.start()

    when(1, send_south)

    def from_north():
        last_row.wait_recv()
        last_cell.wait_recv()
        for h in range(halves):
            grid[h, 0, 7:8, :] = corner[h, 7:8, :]

    def no_north():
        grid[:, 0] = jnp.zeros((halves,) + grid.shape[2:], grid.dtype)

    last_col.wait_recv()
    for h in range(halves):
        for r in range(2 * rows):
            grid[h, 1 + r, 7:8, :] = west[h, r : r + 1, :]
    pl.when(has[-1])(from_north)
    pl.when(lat == 0)(no_north)

    def down_band(p, carry):
        lines = []
        for r in range(STEP):
            i = STEP * p + r
            line = []
            for h in range(halves):
                lanes = slice(h * LANES, (h + 1) * LANES)
                total = jnp.broadcast_to(b_depth[:, lanes], (cols, LANES))
                for a in range(3):
                    for b in range(3):
                        piece = grid[h, 2 * i + a, pl.ds(7 + b, cols, stride=2), :]
                        total = total + piece * w_depth[a, b : b + 1, lanes]
                line.append(total * mask[i][:, :LANES])
            lines.append(jnp.concatenate(line, axis=1))
        for q in range(sectors):
            block = jnp.concatenate([line[STEP * q : STEP * q + STEP] for line in lines], axis=0)
            down[1 + p, 1 + q] = block.astype(down.dtype)
        return carry

    lax.fori_loop(0, bands, down_band, 0)

    def exchange(buffer, width, sems):
        def part(d, count, target):
            if d == 0:
                return slice(width, width + count)
            if (d > 0) != target:
                return slice(count, count + width) if d > 0 else slice(count + width, count + 2 * width)
            return slice(0, width) if target else slice(width, 2 * width)

        copies = []
        for k, (dp, dq) in enumerate(SIDES):
            src = buffer.at[part(dp, bands, False), part(dq, sectors, False)]
            dst = buffer.at[part(dp, bands, True), part(dq, sectors, True)]
            copies.append((dp, remote(src, dst, sems, k, dp, dq)))
        return copies

    def start(copies):
        for dp, copy in copies:
            when(dp, copy.start)

    def arrive(copies):
        for dp, copy in copies:
            when(-dp, copy.wait_recv)

    moves = exchange(down, 1, down_sem)
    start(moves)
    load_one.wait()
    load_two.wait()
    if tail:
        for t in range(9):
            two_tail[t] = jnp.zeros(two_tail.shape[1:], two_tail.dtype)
            two_tail[t, 0:tail, :] = two[t // 3, t % 3, main:feats, :]
    arrive(moves)

    chunk = bands // 2
    flat = chunk * sectors * STEP * STEP

    def first(c, carry):
        p = c * chunk
        pieces = [
            down[pl.ds(p + a, chunk), b : b + sectors].reshape(flat, chans)
            for a in range(3) for b in range(3)
        ]
        total = jnp.dot(
            jnp.concatenate(pieces, axis=1), one[...].reshape(9 * chans, feats),
            preferred_element_type=jnp.float32)
        value = gelu(total + b_one[...]).astype(hidden.dtype)
        hidden[pl.ds(2 + p, chunk), 2 : 2 + sectors, :, 0:feats] = value.reshape(
            chunk, sectors, STEP * STEP, feats)
        return carry

    lax.fori_loop(0, 2, first, 0)

    moves_two = exchange(hidden, 2, hidden_sem)
    start(moves_two)
    arrive(moves_two)

    def second(c, carry):
        p = c * chunk
        taps = [(a, b) for a in range(3) for b in range(3)]
        total = jnp.dot(
            jnp.concatenate(
                [hidden[pl.ds(p + 2 * a, chunk), 2 * b : 2 * b + sectors, :, 0:main].reshape(flat, main)
                 for a, b in taps], axis=1),
            jnp.concatenate([two[a, b, 0:main, :] for a, b in taps], axis=0),
            preferred_element_type=jnp.float32)
        if tail:
            extra = hidden.shape[3] - main
            total = total + jnp.dot(
                jnp.concatenate(
                    [hidden[pl.ds(p + 2 * a, chunk), 2 * b : 2 * b + sectors, :, main:].reshape(flat, extra)
                     for a, b in taps], axis=1),
                two_tail[...].reshape(9 * extra, feats),
                preferred_element_type=jnp.float32)
        value = gelu(total + b_two[...]).reshape(chunk, sectors, STEP * STEP, feats)
        for k in range(chunk):
            for r in range(STEP):
                line = jnp.concatenate(
                    [value[k, q, STEP * r : STEP * r + STEP] for q in range(sectors)], axis=0)
                i = STEP * (p + k) + r
                result[i] = line * mask[i][:, :feats]
        return carry

    lax.fori_loop(0, 2, second, 0)
    store = pltpu.make_async_copy(result, out, out_sem.at[0])
    store.start()

    last_col.wait_send()

    def sent_south():
        last_row.wait_send()
        last_cell.wait_send()

    when(1, sent_south)
    for dp, copy in moves + moves_two:
        when(dp, copy.wait_send)
    store.wait()


def on_device(n_lat, n_lon, fields, land_sea, w_depth, b_depth, w_one, b_one, w_two, b_two):
    rows, cols = land_sea.shape
    chans, feats = w_one.shape[2:]
    bands, sectors = rows // STEP, cols // STEP
    main = feats // (2 * LANES) * (2 * LANES)
    wide = up_to(feats, LANES)
    halves = chans // LANES
    any_space = pl.BlockSpec(memory_space=pl.ANY)
    vmem = pl.BlockSpec(memory_space=pltpu.VMEM)
    return pl.pallas_call(
        functools.partial(kernel, (n_lat, n_lon, rows, cols, chans, feats)),
        out_shape=jax.ShapeDtypeStruct((rows, cols, feats), jnp.float32),
        in_specs=[any_space, vmem, vmem, vmem, any_space, vmem, any_space, vmem],
        out_specs=any_space,
        scratch_shapes=[
            pltpu.VMEM((halves, 2 * rows + 1, 2 * cols + 8, LANES), jnp.float32),
            pltpu.VMEM((halves, 2 * rows, LANES), jnp.float32),
            pltpu.VMEM((halves, 2 * rows, LANES), jnp.float32),
            pltpu.VMEM((halves, 8, LANES), jnp.float32),
            pltpu.VMEM((rows, cols, wide), jnp.float32),
            pltpu.VMEM((bands + 2, sectors + 2, STEP * STEP, chans), jnp.bfloat16),
            pltpu.VMEM((bands + 4, sectors + 4, STEP * STEP, wide), jnp.bfloat16),
            pltpu.VMEM(w_one.shape, jnp.bfloat16),
            pltpu.VMEM(w_two.shape, jnp.bfloat16),
            pltpu.VMEM((9, max(wide - main, LANES), feats), jnp.bfloat16),
            pltpu.VMEM((rows, cols, feats), jnp.float32),
            pltpu.SemaphoreType.DMA((2 + halves,)),
            pltpu.SemaphoreType.DMA((2, 3)),
            pltpu.SemaphoreType.DMA((2, len(SIDES))),
            pltpu.SemaphoreType.DMA((2, len(SIDES))),
            pltpu.SemaphoreType.DMA((1,)),
        ],
        compiler_params=pltpu.CompilerParams(
            collective_id=0, has_side_effects=True, vmem_limit_bytes=40 * 1024 * 1024),
    )(fields, land_sea, w_depth, b_depth.reshape(1, chans), w_one, b_one.reshape(1, feats),
      w_two, b_two.reshape(1, feats))


def solution(mesh):
    return jax.shard_map(
        functools.partial(on_device, mesh.shape["lat"], mesh.shape["lon"]),
        mesh=mesh,
        in_specs=(P("lat", "lon", None), P("lat", "lon"), P(), P(), P(), P(), P(), P()),
        out_specs=P("lat", "lon", None),
        check_vma=False,
    )
```

```python
import functools

import jax
import jax.numpy as jnp
from jax import lax
from jax.experimental import pallas as pl
from jax.experimental.pallas import tpu as pltpu
from jax.sharding import PartitionSpec as P

MESH = pl.DeviceIdType.MESH
SIDES = tuple((dp, dq) for dp in (-1, 0, 1) for dq in (-1, 0, 1) if (dp, dq) != (0, 0))
STEP = 4
LANES = 128


def gelu(x):
    return 0.5 * x * (1.0 + lax.erf(x * 0.7071067811865476))


def up_to(value, multiple):
    return -(-value // multiple) * multiple


def kernel(
    shape, fields, land, w_depth, b_depth, w_one, b_one, w_two, b_two, out,
    grid, edge, west, corner, late, open_block, open_sea, mask, down, hidden, one, two, two_tail, result,
    load_sem, edge_sem, down_sem, hidden_sem, out_sem,
):
    n_lat, n_lon, rows, cols, chans, feats = shape
    bands, sectors = rows // STEP, cols // STEP
    main = feats // (2 * LANES) * (2 * LANES)
    tail = feats - main
    lat, lon = lax.axis_index("lat"), lax.axis_index("lon")
    has = {-1: lat > 0, 0: True, 1: lat < n_lat - 1}

    def when(dp, body):
        if dp == 0:
            body()
        else:
            pl.when(has[dp])(body)

    def device(dp, dq):
        return (lat + dp, lax.rem(lon + dq + n_lon, n_lon))

    halves = chans // LANES
    parts = [
        pltpu.make_async_copy(
            fields.at[:, :, h * LANES : (h + 1) * LANES], grid.at[h, 1:, 8:, :], load_sem.at[2 + h])
        for h in range(halves)
    ]
    load_one = pltpu.make_async_copy(w_one, one, load_sem.at[0])
    load_two = pltpu.make_async_copy(w_two, two, load_sem.at[1])
    for load in parts + [load_one, load_two]:
        load.start()

    barrier = pltpu.get_barrier_semaphore()
    for dp, dq in SIDES:
        when(dp, lambda dp=dp, dq=dq: pl.semaphore_signal(
            barrier, inc=1, device_id=device(dp, dq), device_id_type=MESH))

    cells = land[...].astype(jnp.float32)
    for i in range(rows):
        mask[i] = jnp.broadcast_to(cells[:, i : i + 1], mask.shape[1:])

    if tail:
        hidden[:, :, :, main:] = jnp.zeros(hidden.shape[:3] + (hidden.shape[3] - main,), hidden.dtype)

    def clear(buffer, width):
        gap = jnp.zeros((width,) + buffer.shape[1:], buffer.dtype)

        def north():
            buffer[0:width] = gap

        def south():
            buffer[buffer.shape[0] - width :] = gap

        pl.when(lat == 0)(north)
        pl.when(lat == n_lat - 1)(south)

    def no_north():
        grid[:, 0, 8:, :] = jnp.zeros((halves, 2 * cols, LANES), grid.dtype)

    pl.when(lat == 0)(no_north)
    clear(down, 1)
    clear(hidden, 2)

    for h in range(halves):
        parts[h].wait()
        for r in range(2 * rows):
            edge[h, r : r + 1, :] = grid[h, 1 + r, 8 + 2 * cols - 1 : 8 + 2 * cols, :]

    pl.semaphore_wait(barrier, 2 + 3 * jnp.minimum(lat, 1) + 3 * jnp.minimum(n_lat - 1 - lat, 1))

    def remote(src, dst, sems, k, dp, dq):
        return pltpu.make_async_remote_copy(
            src_ref=src, dst_ref=dst, send_sem=sems.at[0, k], recv_sem=sems.at[1, k],
            device_id=device(dp, dq), device_id_type=MESH)

    last_row = remote(grid.at[:, 2 * rows, 8:, :], grid.at[:, 0, 8:, :], edge_sem, 0, 1, 0)
    last_col = remote(edge, west, edge_sem, 1, 0, 1)
    last_cell = remote(edge.at[:, 2 * rows - 8 :], corner, edge_sem, 2, 1, 1)
    last_col.start()

    def send_south():
        last_row.start()
        last_cell.start()

    when(1, send_south)

    def from_north():
        last_row.wait_recv()
        last_cell.wait_recv()
        for h in range(halves):
            grid[h, 0, 7:8, :] = corner[h, 7:8, :]

    def no_north():
        grid[:, 0] = jnp.zeros((halves,) + grid.shape[2:], grid.dtype)

    for h in range(halves):
        grid[h, :, 0:8, :] = jnp.zeros((2 * rows + 1, 8, LANES), grid.dtype)
        late[h] = jnp.zeros(late.shape[1:], late.dtype)

    def down_line(i):
        line = []
        for h in range(halves):
            lanes = slice(h * LANES, (h + 1) * LANES)
            total = jnp.broadcast_to(b_depth[...].reshape(1, chans)[:, lanes], (cols, LANES))
            for a in range(3):
                for b in range(3):
                    piece = grid[h, 2 * i + a, pl.ds(7 + b, cols, stride=2), :]
                    total = total + piece * w_depth[a, b : b + 1, lanes]
            line.append(total)
        return jnp.concatenate(line, axis=1)

    def gather(lines, q):
        return jnp.concatenate([line[STEP * q : STEP * q + STEP] for line in lines], axis=0)

    def down_band(p):
        lines = [down_line(STEP * p + r) for r in range(STEP)]
        seas = [mask[STEP * p + r][:, :chans] for r in range(STEP)]
        masked = [line * sea for line, sea in zip(lines, seas)]
        for q in range(1, sectors):
            down[1 + p, 1 + q] = gather(masked, q).astype(down.dtype)
        return gather(lines, 0), gather(seas, 0)

    def later_band(p, carry):
        block, sea = down_band(p)
        open_block[p] = block
        open_sea[p] = sea
        return carry

    lax.fori_loop(1, bands, later_band, 0)

    last_col.wait_recv()
    for h in range(halves):
        lanes = slice(h * LANES, (h + 1) * LANES)
        from_west = sum(
            west[h, pl.ds(8 * STEP // 4 - 1 + a, rows - STEP, stride=2), :] * w_depth[a, 0:1, lanes]
            for a in range(3))
        late[h, pl.ds(STEP * STEP, rows - STEP, stride=STEP), :] = from_west
    for p in range(1, bands):
        extra = jnp.concatenate(
            [late[h, STEP * STEP * p : STEP * STEP * (p + 1), :] for h in range(halves)], axis=1)
        down[1 + p, 1] = ((open_block[p] + extra) * open_sea[p]).astype(down.dtype)

    def from_north():
        last_row.wait_recv()
        last_cell.wait_recv()
        for h in range(halves):
            grid[h, 0, 7:8, :] = corner[h, 7:8, :]

    for h in range(halves):
        for r in range(2 * STEP):
            grid[h, 1 + r, 7:8, :] = west[h, r : r + 1, :]
    pl.when(has[-1])(from_north)
    block, sea = down_band(0)
    down[1, 1] = (block * sea).astype(down.dtype)

    def exchange(buffer, width, sems):
        def part(d, count, target):
            if d == 0:
                return slice(width, width + count)
            if (d > 0) != target:
                return slice(count, count + width) if d > 0 else slice(count + width, count + 2 * width)
            return slice(0, width) if target else slice(width, 2 * width)

        copies = []
        for k, (dp, dq) in enumerate(SIDES):
            src = buffer.at[part(dp, bands, False), part(dq, sectors, False)]
            dst = buffer.at[part(dp, bands, True), part(dq, sectors, True)]
            copies.append((dp, remote(src, dst, sems, k, dp, dq)))
        return copies

    def start(copies):
        for dp, copy in copies:
            when(dp, copy.start)

    def arrive(copies):
        for dp, copy in copies:
            when(-dp, copy.wait_recv)

    moves = exchange(down, 1, down_sem)
    start(moves)
    load_one.wait()
    load_two.wait()
    if tail:
        for t in range(9):
            two_tail[t] = jnp.zeros(two_tail.shape[1:], two_tail.dtype)
            two_tail[t, 0:tail, :] = two[t // 3, t % 3, main:feats, :]
    arrive(moves)

    chunk = bands // 2
    flat = chunk * sectors * STEP * STEP

    def first(c, carry):
        p = c * chunk
        pieces = [
            down[pl.ds(p + a, chunk), b : b + sectors].reshape(flat, chans)
            for a in range(3) for b in range(3)
        ]
        total = lax.dot_general(
            jnp.concatenate(pieces, axis=1),
            jnp.concatenate([one[a, b] for a in range(3) for b in range(3)], axis=1),
            (((1,), (1,)), ((), ())), preferred_element_type=jnp.float32)
        value = gelu(total + b_one[...].reshape(1, feats)).astype(hidden.dtype)
        hidden[pl.ds(2 + p, chunk), 2 : 2 + sectors, :, 0:feats] = value.reshape(
            chunk, sectors, STEP * STEP, feats)
        return carry

    lax.fori_loop(0, 2, first, 0)

    moves_two = exchange(hidden, 2, hidden_sem)
    start(moves_two)
    arrive(moves_two)

    def second(c, carry):
        p = c * chunk
        taps = [(a, b) for a in range(3) for b in range(3)]
        total = jnp.dot(
            jnp.concatenate(
                [hidden[pl.ds(p + 2 * a, chunk), 2 * b : 2 * b + sectors, :, 0:main].reshape(flat, main)
                 for a, b in taps], axis=1),
            jnp.concatenate([two[a, b, 0:main, :] for a, b in taps], axis=0),
            preferred_element_type=jnp.float32)
        if tail:
            extra = hidden.shape[3] - main
            total = total + jnp.dot(
                jnp.concatenate(
                    [hidden[pl.ds(p + 2 * a, chunk), 2 * b : 2 * b + sectors, :, main:].reshape(flat, extra)
                     for a, b in taps], axis=1),
                two_tail[...].reshape(9 * extra, feats),
                preferred_element_type=jnp.float32)
        value = gelu(total + b_two[...].reshape(1, feats)).reshape(chunk, sectors, STEP * STEP, feats)
        for k in range(chunk):
            for r in range(STEP):
                line = jnp.concatenate(
                    [value[k, q, STEP * r : STEP * r + STEP] for q in range(sectors)], axis=0)
                i = STEP * (p + k) + r
                result[i] = line * mask[i][:, :feats]
        return carry

    lax.fori_loop(0, 2, second, 0)
    store = pltpu.make_async_copy(result, out, out_sem.at[0])
    store.start()

    last_col.wait_send()

    def sent_south():
        last_row.wait_send()
        last_cell.wait_send()

    when(1, sent_south)
    for dp, copy in moves + moves_two:
        when(dp, copy.wait_send)
    store.wait()


def on_device(n_lat, n_lon, fields, land_sea, w_depth, b_depth, w_one, b_one, w_two, b_two):
    rows, cols = land_sea.shape
    chans, feats = w_one.shape[2:]
    bands, sectors = rows // STEP, cols // STEP
    main = feats // (2 * LANES) * (2 * LANES)
    wide = up_to(feats, LANES)
    halves = chans // LANES
    taps_out_in = jnp.swapaxes(w_one, 2, 3)
    any_space = pl.BlockSpec(memory_space=pl.ANY)
    vmem = pl.BlockSpec(memory_space=pltpu.VMEM)
    return pl.pallas_call(
        functools.partial(kernel, (n_lat, n_lon, rows, cols, chans, feats)),
        out_shape=jax.ShapeDtypeStruct((rows, cols, feats), jnp.float32),
        in_specs=[any_space, vmem, vmem, vmem, any_space, vmem, any_space, vmem],
        out_specs=any_space,
        scratch_shapes=[
            pltpu.VMEM((halves, 2 * rows + 1, 2 * cols + 8, LANES), jnp.float32),
            pltpu.VMEM((halves, 2 * rows, LANES), jnp.float32),
            pltpu.VMEM((halves, 2 * rows, LANES), jnp.float32),
            pltpu.VMEM((halves, 8, LANES), jnp.float32),
            pltpu.VMEM((halves, STEP * rows, LANES), jnp.float32),
            pltpu.VMEM((bands, STEP * STEP, chans), jnp.float32),
            pltpu.VMEM((bands, STEP * STEP, chans), jnp.float32),
            pltpu.VMEM((rows, cols, wide), jnp.float32),
            pltpu.VMEM((bands + 2, sectors + 2, STEP * STEP, chans), jnp.bfloat16),
            pltpu.VMEM((bands + 4, sectors + 4, STEP * STEP, wide), jnp.bfloat16),
            pltpu.VMEM(taps_out_in.shape, jnp.bfloat16),
            pltpu.VMEM(w_two.shape, jnp.bfloat16),
            pltpu.VMEM((9, max(wide - main, LANES), feats), jnp.bfloat16),
            pltpu.VMEM((rows, cols, feats), jnp.float32),
            pltpu.SemaphoreType.DMA((2 + halves,)),
            pltpu.SemaphoreType.DMA((2, 3)),
            pltpu.SemaphoreType.DMA((2, len(SIDES))),
            pltpu.SemaphoreType.DMA((2, len(SIDES))),
            pltpu.SemaphoreType.DMA((1,)),
        ],
        compiler_params=pltpu.CompilerParams(
            collective_id=0, has_side_effects=True, vmem_limit_bytes=62 * 1024 * 1024),
    )(fields, land_sea.T, w_depth, b_depth, taps_out_in, b_one, w_two, b_two)


def solution(mesh):
    return jax.shard_map(
        functools.partial(on_device, mesh.shape["lat"], mesh.shape["lon"]),
        mesh=mesh,
        in_specs=(P("lat", "lon", None), P("lat", "lon"), P(), P(), P(), P(), P(), P()),
        out_specs=P("lat", "lon", None),
        check_vma=False,
    )
```

```python
import functools

import jax
import jax.numpy as jnp
from jax import lax
from jax.experimental import pallas as pl
from jax.experimental.pallas import tpu as pltpu
from jax.sharding import PartitionSpec as P

MESH = pl.DeviceIdType.MESH
SIDES = tuple((dp, dq) for dp in (-1, 0, 1) for dq in (-1, 0, 1) if (dp, dq) != (0, 0))
STEP = 4
LANES = 128


def gelu(x):
    return 0.5 * x * (1.0 + lax.erf(x * 0.7071067811865476))


def up_to(value, multiple):
    return -(-value // multiple) * multiple


def kernel(
    shape, fields, land, w_depth, b_depth, w_one, b_one, w_two, b_two, out,
    grid, edge, west, corner, late, open_block, open_sea, mask, down, hidden, one, two, two_tail, from_n, from_s, from_w, from_e, sums,
    load_sem, edge_sem, down_sem, hidden_sem,
):
    n_lat, n_lon, rows, cols, chans, feats = shape
    bands, sectors = rows // STEP, cols // STEP
    main = feats // (2 * LANES) * (2 * LANES)
    tail = feats - main
    lat, lon = lax.axis_index("lat"), lax.axis_index("lon")
    has = {-1: lat > 0, 0: True, 1: lat < n_lat - 1}

    def when(dp, body):
        if dp == 0:
            body()
        else:
            pl.when(has[dp])(body)

    def device(dp, dq):
        return (lat + dp, lax.rem(lon + dq + n_lon, n_lon))

    halves = chans // LANES
    split = 2 * cols - 8

    def part(h, k):
        start, size = ((split, 8), (0, split))[k]
        return pltpu.make_async_copy(
            fields.at[:, start : start + size, h * LANES : (h + 1) * LANES],
            grid.at[h, 1:, 8 + start : 8 + start + size, :], load_sem.at[2 + 2 * h + k])

    edge_parts = [part(h, 0) for h in range(halves)]
    inner_parts = [part(h, 1) for h in range(halves)]
    load_one = pltpu.make_async_copy(w_one, one, load_sem.at[0])
    load_two = pltpu.make_async_copy(w_two, two, load_sem.at[1])
    for load in edge_parts + inner_parts:
        load.start()

    barrier = pltpu.get_barrier_semaphore()
    for dp, dq in SIDES:
        when(dp, lambda dp=dp, dq=dq: pl.semaphore_signal(
            barrier, inc=1, device_id=device(dp, dq), device_id_type=MESH))

    cells = land[...].astype(jnp.float32)
    for i in range(rows):
        mask[i] = jnp.broadcast_to(cells[:, i : i + 1], mask.shape[1:])

    for p in range(bands + 4):
        hidden[p] = jnp.zeros(hidden.shape[1:], hidden.dtype)

    def clear(buffer, width):
        gap = jnp.zeros((width,) + buffer.shape[1:], buffer.dtype)

        def north():
            buffer[0:width] = gap

        def south():
            buffer[buffer.shape[0] - width :] = gap

        pl.when(lat == 0)(north)
        pl.when(lat == n_lat - 1)(south)

    def no_north():
        grid[:, 0, 8:, :] = jnp.zeros((halves, 2 * cols, LANES), grid.dtype)

    pl.when(lat == 0)(no_north)
    clear(down, 1)

    def clear_far(lat_at, first, line):
        def body():
            for buffer in (from_w, from_e):
                buffer[first : first + 2] = jnp.zeros((2,) + buffer.shape[1:], buffer.dtype)
            line[:, 2 : 2 + sectors] = jnp.zeros((2, sectors) + line.shape[2:], line.dtype)

        pl.when(lat == lat_at)(body)

    clear_far(0, 0, from_n)
    clear_far(n_lat - 1, bands + 2, from_s)
    for line in (from_n, from_s):
        for q in (0, 2 + sectors):
            line[:, q : q + 2] = jnp.zeros((2, 2) + line.shape[2:], line.dtype)

    for h in range(halves):
        edge_parts[h].wait()
        for r in range(2 * rows):
            edge[h, r : r + 1, :] = grid[h, 1 + r, 8 + 2 * cols - 1 : 8 + 2 * cols, :]

    pl.semaphore_wait(barrier, 2 + 3 * jnp.minimum(lat, 1) + 3 * jnp.minimum(n_lat - 1 - lat, 1))

    def remote(src, dst, sems, k, dp, dq):
        return pltpu.make_async_remote_copy(
            src_ref=src, dst_ref=dst, send_sem=sems.at[0, k], recv_sem=sems.at[1, k],
            device_id=device(dp, dq), device_id_type=MESH)

    last_row = remote(grid.at[:, 2 * rows, 8:, :], grid.at[:, 0, 8:, :], edge_sem, 0, 1, 0)
    last_col = remote(edge, west, edge_sem, 1, 0, 1)
    last_cell = remote(edge.at[:, 2 * rows - 8 :], corner, edge_sem, 2, 1, 1)
    last_col.start()
    when(1, last_cell.start)
    for inner in inner_parts:
        inner.wait()
    when(1, last_row.start)
    load_one.start()
    load_two.start()

    def from_north():
        last_row.wait_recv()
        last_cell.wait_recv()
        for h in range(halves):
            grid[h, 0, 7:8, :] = corner[h, 7:8, :]

    def no_north():
        grid[:, 0] = jnp.zeros((halves,) + grid.shape[2:], grid.dtype)

    for h in range(halves):
        grid[h, :, 0:8, :] = jnp.zeros((2 * rows + 1, 8, LANES), grid.dtype)
        late[h] = jnp.zeros(late.shape[1:], late.dtype)

    def down_line(i):
        line = []
        for h in range(halves):
            lanes = slice(h * LANES, (h + 1) * LANES)
            total = jnp.broadcast_to(b_depth[...].reshape(1, chans)[:, lanes], (cols, LANES))
            for a in range(3):
                for b in range(3):
                    piece = grid[h, 2 * i + a, pl.ds(7 + b, cols, stride=2), :]
                    total = total + piece * w_depth[a, b : b + 1, lanes]
            line.append(total)
        return jnp.concatenate(line, axis=1)

    def gather(lines, q):
        return jnp.concatenate([line[STEP * q : STEP * q + STEP] for line in lines], axis=0)

    def down_band(p):
        lines = [down_line(STEP * p + r) for r in range(STEP)]
        seas = [mask[STEP * p + r][:, :chans] for r in range(STEP)]
        masked = [line * sea for line, sea in zip(lines, seas)]
        for q in range(1, sectors):
            down[1 + p, 1 + q] = gather(masked, q).astype(down.dtype)
        return gather(lines, 0), gather(seas, 0)

    def later_band(p, carry):
        block, sea = down_band(p)
        open_block[p] = block
        open_sea[p] = sea
        return carry

    lax.fori_loop(1, bands, later_band, 0)

    last_col.wait_recv()
    for h in range(halves):
        lanes = slice(h * LANES, (h + 1) * LANES)
        from_west = sum(
            west[h, pl.ds(8 * STEP // 4 - 1 + a, rows - STEP, stride=2), :] * w_depth[a, 0:1, lanes]
            for a in range(3))
        late[h, pl.ds(STEP * STEP, rows - STEP, stride=STEP), :] = from_west
    for p in range(1, bands):
        extra = jnp.concatenate(
            [late[h, STEP * STEP * p : STEP * STEP * (p + 1), :] for h in range(halves)], axis=1)
        down[1 + p, 1] = ((open_block[p] + extra) * open_sea[p]).astype(down.dtype)

    def from_north():
        last_row.wait_recv()
        last_cell.wait_recv()
        for h in range(halves):
            grid[h, 0, 7:8, :] = corner[h, 7:8, :]

    for h in range(halves):
        for r in range(2 * STEP):
            grid[h, 1 + r, 7:8, :] = west[h, r : r + 1, :]
    pl.when(has[-1])(from_north)
    block, sea = down_band(0)
    down[1, 1] = (block * sea).astype(down.dtype)

    def exchange(buffer, width, sems):
        def part(d, count, target):
            if d == 0:
                return slice(width, width + count)
            if (d > 0) != target:
                return slice(count, count + width) if d > 0 else slice(count + width, count + 2 * width)
            return slice(0, width) if target else slice(width, 2 * width)

        copies = []
        for k, (dp, dq) in enumerate(SIDES):
            src = buffer.at[part(dp, bands, False), part(dq, sectors, False)]
            dst = buffer.at[part(dp, bands, True), part(dq, sectors, True)]
            copies.append((dp, remote(src, dst, sems, k, dp, dq)))
        return copies

    def start(copies):
        for dp, copy in copies:
            when(dp, copy.start)

    def arrive(copies):
        for dp, copy in copies:
            when(-dp, copy.wait_recv)

    moves = exchange(down, 1, down_sem)
    start(moves)
    load_one.wait()
    load_two.wait()
    if tail:
        for t in range(9):
            two_tail[t] = jnp.zeros(two_tail.shape[1:], two_tail.dtype)
            two_tail[t, 0:tail, :] = two[t // 3, t % 3, main:feats, :]
    arrive(moves)

    chunk = bands // 2
    flat = chunk * sectors * STEP * STEP

    def first(c, carry):
        p = c * chunk
        pieces = [
            down[pl.ds(p + a, chunk), b : b + sectors].reshape(flat, chans)
            for a in range(3) for b in range(3)
        ]
        total = lax.dot_general(
            jnp.concatenate(pieces, axis=1),
            jnp.concatenate([one[a, b] for a in range(3) for b in range(3)], axis=1),
            (((1,), (1,)), ((), ())), preferred_element_type=jnp.float32)
        value = gelu(total + b_one[...].reshape(1, feats)).astype(hidden.dtype)
        hidden[pl.ds(2 + p, chunk), 2 : 2 + sectors, :, 0:feats] = value.reshape(
            chunk, sectors, STEP * STEP, feats)
        return carry

    lax.fori_loop(0, 2, first, 0)

    def side(k, dq, first, count):
        buffer, q = (from_w, 2 + sectors - 2) if dq > 0 else (from_e, 2)
        return remote(hidden.at[2 + first : 2 + first + count, q : q + 2],
                      buffer.at[2 + first : 2 + first + count], hidden_sem, k, 0, dq)

    outer = [side(0, 1, 0, 2), side(1, -1, 0, 2), side(2, 1, bands - 2, 2), side(3, -1, bands - 2, 2)]
    inner = [side(4, 1, 2, bands - 4), side(5, -1, 2, bands - 4)]
    own = slice(2, 2 + sectors)
    lat_moves = [
        (-1, remote(hidden.at[2:4, own], from_s.at[:, own], hidden_sem, 6, -1, 0)),
        (1, remote(hidden.at[bands : bands + 2, own], from_n.at[:, own], hidden_sem, 7, 1, 0)),
    ]
    corners = [
        (-1, remote(from_w.at[2:4], from_w.at[bands + 2 :], hidden_sem, 8, -1, 0)),
        (-1, remote(from_e.at[2:4], from_e.at[bands + 2 :], hidden_sem, 9, -1, 0)),
        (1, remote(from_w.at[bands : bands + 2], from_w.at[0:2], hidden_sem, 10, 1, 0)),
        (1, remote(from_e.at[bands : bands + 2], from_e.at[0:2], hidden_sem, 11, 1, 0)),
    ]
    for copy in outer:
        copy.start()
    start(lat_moves)
    for copy in inner:
        copy.start()

    def taps_of(buffer, places, taps, size):
        count = size[0] * size[1] * STEP * STEP
        window = [
            buffer[pl.ds(p, size[0]), q : q + size[1]].reshape(count, buffer.shape[3])
            for p, q in places
        ]
        total = jnp.dot(
            jnp.concatenate([cells[:, 0:main] for cells in window], axis=1),
            jnp.concatenate([two[a, b, 0:main, :] for a, b in taps], axis=0),
            preferred_element_type=jnp.float32)
        if tail:
            total = total + jnp.dot(
                jnp.concatenate([cells[:, main:] for cells in window], axis=1),
                jnp.concatenate([two_tail[3 * a + b] for a, b in taps], axis=0),
                preferred_element_type=jnp.float32)
        return total.reshape(size + (STEP * STEP, feats))

    every = [(a, b) for a in range(3) for b in range(3)]

    def second(c):
        p = c * chunk
        sums[p : p + chunk] = taps_of(
            hidden, [(p + 2 * a, 2 * b) for a, b in every], every, (chunk, sectors))

    second(0)
    for copy in outer:
        copy.wait_recv()
    start(corners)
    second(1)
    arrive(lat_moves)
    sums[0:2] += taps_of(from_n, [(0, 2 * b) for b in range(3)], [(0, b) for b in range(3)], (2, sectors))
    sums[bands - 2 :] += taps_of(
        from_s, [(0, 2 * b) for b in range(3)], [(2, b) for b in range(3)], (2, sectors))
    for copy in inner:
        copy.wait_recv()
    arrive(corners)
    sums[:, 0:2] += taps_of(from_w, [(2 * a, 0) for a in range(3)], [(a, 0) for a in range(3)], (bands, 2))
    sums[:, sectors - 2 :] += taps_of(
        from_e, [(2 * a, 0) for a in range(3)], [(a, 2) for a in range(3)], (bands, 2))

    def finish(p, carry):
        value = gelu(sums[p] + b_two[...].reshape(1, 1, feats))
        for r in range(STEP):
            i = STEP * p + r
            out[i] = gather([value[q, STEP * r : STEP * r + STEP] for q in range(sectors)], 0) * mask[i][:, :feats]
        return carry

    lax.fori_loop(0, bands, finish, 0)

    last_col.wait_send()

    def sent_south():
        last_row.wait_send()
        last_cell.wait_send()

    when(1, sent_south)
    for dp, copy in moves + lat_moves + corners:
        when(dp, copy.wait_send)
    for copy in outer + inner:
        copy.wait_send()


def on_device(n_lat, n_lon, fields, land_sea, w_depth, b_depth, w_one, b_one, w_two, b_two):
    rows, cols = land_sea.shape
    chans, feats = w_one.shape[2:]
    bands, sectors = rows // STEP, cols // STEP
    main = feats // (2 * LANES) * (2 * LANES)
    wide = up_to(feats, LANES)
    halves = chans // LANES
    taps_out_in = jnp.swapaxes(w_one, 2, 3)
    any_space = pl.BlockSpec(memory_space=pltpu.HBM)
    vmem = pl.BlockSpec(memory_space=pltpu.VMEM)
    return pl.pallas_call(
        functools.partial(kernel, (n_lat, n_lon, rows, cols, chans, feats)),
        out_shape=pltpu.VMEM((rows, cols, feats), jnp.float32),
        in_specs=[any_space, vmem, vmem, vmem, any_space, vmem, any_space, vmem],
        out_specs=vmem,
        scratch_shapes=[
            pltpu.VMEM((halves, 2 * rows + 1, 2 * cols + 8, LANES), jnp.float32),
            pltpu.VMEM((halves, 2 * rows, LANES), jnp.float32),
            pltpu.VMEM((halves, 2 * rows, LANES), jnp.float32),
            pltpu.VMEM((halves, 8, LANES), jnp.float32),
            pltpu.VMEM((halves, STEP * rows, LANES), jnp.float32),
            pltpu.VMEM((bands, STEP * STEP, chans), jnp.float32),
            pltpu.VMEM((bands, STEP * STEP, chans), jnp.float32),
            pltpu.VMEM((rows, cols, wide), jnp.float32),
            pltpu.VMEM((bands + 2, sectors + 2, STEP * STEP, chans), jnp.bfloat16),
            pltpu.VMEM((bands + 4, sectors + 4, STEP * STEP, wide), jnp.bfloat16),
            pltpu.VMEM(taps_out_in.shape, jnp.bfloat16),
            pltpu.VMEM(w_two.shape, jnp.bfloat16),
            pltpu.VMEM((9, max(wide - main, LANES), feats), jnp.bfloat16),
            pltpu.VMEM((2, sectors + 4, STEP * STEP, wide), jnp.bfloat16),
            pltpu.VMEM((2, sectors + 4, STEP * STEP, wide), jnp.bfloat16),
            pltpu.VMEM((bands + 4, 2, STEP * STEP, wide), jnp.bfloat16),
            pltpu.VMEM((bands + 4, 2, STEP * STEP, wide), jnp.bfloat16),
            pltpu.VMEM((bands, sectors, STEP * STEP, feats), jnp.float32),
            pltpu.SemaphoreType.DMA((2 + 2 * halves,)),
            pltpu.SemaphoreType.DMA((2, 3)),
            pltpu.SemaphoreType.DMA((2, len(SIDES))),
            pltpu.SemaphoreType.DMA((2, 12)),
        ],
        compiler_params=pltpu.CompilerParams(
            collective_id=0, has_side_effects=True, vmem_limit_bytes=62 * 1024 * 1024),
    )(fields, land_sea.T, w_depth, b_depth, taps_out_in, b_one, w_two, b_two)


def solution(mesh):
    return jax.shard_map(
        functools.partial(on_device, mesh.shape["lat"], mesh.shape["lon"]),
        mesh=mesh,
        in_specs=(P("lat", "lon", None), P("lat", "lon"), P(), P(), P(), P(), P(), P()),
        out_specs=P("lat", "lon", None),
        check_vma=False,
    )
```

```python
import functools

import jax
import jax.numpy as jnp
from jax import lax
from jax.experimental import pallas as pl
from jax.experimental.pallas import tpu as pltpu
from jax.sharding import PartitionSpec as P

MESH = pl.DeviceIdType.MESH
SIDES = tuple((dp, dq) for dp in (-1, 0, 1) for dq in (-1, 0, 1) if (dp, dq) != (0, 0))
STEP = 4
LANES = 128


def gelu(x):
    return 0.5 * x * (1.0 + lax.erf(x * 0.7071067811865476))


def up_to(value, multiple):
    return -(-value // multiple) * multiple


def kernel(
    shape, fields, land, w_depth, b_depth, w_one, b_one, w_two, b_two, out,
    grid, edge, west, corner, late, open_block, open_sea, mask, down, hidden, one, two, two_tail, sums,
    load_sem, edge_sem, down_sem,
):
    n_lat, n_lon, rows, cols, chans, feats = shape
    bands, sectors = rows // STEP, cols // STEP
    main = feats // (2 * LANES) * (2 * LANES)
    tail = feats - main
    lat, lon = lax.axis_index("lat"), lax.axis_index("lon")
    has = {-1: lat > 0, 0: True, 1: lat < n_lat - 1}

    def when(dp, body):
        if dp == 0:
            body()
        else:
            pl.when(has[dp])(body)

    def device(dp, dq):
        return (lat + dp, lax.rem(lon + dq + n_lon, n_lon))

    halves = chans // LANES
    split = 2 * cols - 8

    def part(h, k):
        start, size = ((split, 8), (0, split))[k]
        return pltpu.make_async_copy(
            fields.at[:, start : start + size, h * LANES : (h + 1) * LANES],
            grid.at[h, 1:, 8 + start : 8 + start + size, :], load_sem.at[2 + 2 * h + k])

    edge_parts = [part(h, 0) for h in range(halves)]
    inner_parts = [part(h, 1) for h in range(halves)]
    load_one = pltpu.make_async_copy(w_one, one, load_sem.at[0])
    load_two = pltpu.make_async_copy(w_two, two, load_sem.at[1])
    for load in edge_parts + inner_parts:
        load.start()

    barrier = pltpu.get_barrier_semaphore()
    for dp, dq in SIDES:
        when(dp, lambda dp=dp, dq=dq: pl.semaphore_signal(
            barrier, inc=1, device_id=device(dp, dq), device_id_type=MESH))

    cells = land[...].astype(jnp.float32)
    for i in range(rows):
        mask[i] = jnp.broadcast_to(cells[:, i : i + 1], mask.shape[1:])

    for p in range(bands + 4):
        hidden[p] = jnp.zeros(hidden.shape[1:], hidden.dtype)

    def clear(buffer, width):
        gap = jnp.zeros((width,) + buffer.shape[1:], buffer.dtype)

        def north():
            buffer[0:width] = gap

        def south():
            buffer[buffer.shape[0] - width :] = gap

        pl.when(lat == 0)(north)
        pl.when(lat == n_lat - 1)(south)

    def no_north():
        grid[:, 0, 8:, :] = jnp.zeros((halves, 2 * cols, LANES), grid.dtype)

    pl.when(lat == 0)(no_north)
    clear(down, 3)

    for h in range(halves):
        edge_parts[h].wait()
        for r in range(2 * rows):
            edge[h, r : r + 1, :] = grid[h, 1 + r, 8 + 2 * cols - 1 : 8 + 2 * cols, :]

    pl.semaphore_wait(barrier, 2 + 3 * jnp.minimum(lat, 1) + 3 * jnp.minimum(n_lat - 1 - lat, 1))

    def remote(src, dst, sems, k, dp, dq):
        return pltpu.make_async_remote_copy(
            src_ref=src, dst_ref=dst, send_sem=sems.at[0, k], recv_sem=sems.at[1, k],
            device_id=device(dp, dq), device_id_type=MESH)

    last_row = remote(grid.at[:, 2 * rows, 8:, :], grid.at[:, 0, 8:, :], edge_sem, 0, 1, 0)
    last_col = remote(edge, west, edge_sem, 1, 0, 1)
    last_cell = remote(edge.at[:, 2 * rows - 8 :], corner, edge_sem, 2, 1, 1)
    last_col.start()
    when(1, last_cell.start)
    for inner in inner_parts:
        inner.wait()
    when(1, last_row.start)
    load_one.start()
    load_two.start()

    for h in range(halves):
        grid[h, :, 0:8, :] = jnp.zeros((2 * rows + 1, 8, LANES), grid.dtype)
        late[h] = jnp.zeros(late.shape[1:], late.dtype)

    def down_line(i):
        line = []
        for h in range(halves):
            lanes = slice(h * LANES, (h + 1) * LANES)
            total = jnp.broadcast_to(b_depth[...].reshape(1, chans)[:, lanes], (cols, LANES))
            for a in range(3):
                for b in range(3):
                    piece = grid[h, 2 * i + a, pl.ds(7 + b, cols, stride=2), :]
                    total = total + piece * w_depth[a, b : b + 1, lanes]
            line.append(total)
        return jnp.concatenate(line, axis=1)

    def gather(lines, q):
        return jnp.concatenate([line[STEP * q : STEP * q + STEP] for line in lines], axis=0)

    def down_band(p):
        lines = [down_line(STEP * p + r) for r in range(STEP)]
        seas = [mask[STEP * p + r][:, :chans] for r in range(STEP)]
        masked = [line * sea for line, sea in zip(lines, seas)]
        for q in range(1, sectors):
            down[3 + p, 3 + q] = gather(masked, q).astype(down.dtype)
        return gather(lines, 0), gather(seas, 0)

    def later_band(p, carry):
        block, sea = down_band(p)
        open_block[p] = block
        open_sea[p] = sea
        return carry

    def halo(k, dp, dq, p, count, q, wide):
        src = down.at[3 + p : 3 + p + count, 3 + q : 3 + q + wide]
        to_p, to_q = 3 + p - dp * bands, 3 + q - dq * sectors
        dst = down.at[to_p : to_p + count, to_q : to_q + wide]
        return dp, remote(src, dst, down_sem, k, dp, dq)

    far = bands - 3
    east = [halo(0, 0, 1, far, 3, sectors - 3, 3), halo(1, 0, 1, 1, far - 1, sectors - 3, 3)]
    west_side = [halo(2, 0, -1, far, 3, 0, 3), halo(3, 0, -1, 1, far - 1, 0, 3)]
    south = [halo(4, 1, 0, far, 3, 0, sectors)]
    top = [halo(5, 0, 1, 0, 1, sectors - 3, 3), halo(6, 0, -1, 0, 1, 0, 3)]
    north = [halo(7, -1, 0, 0, 3, 0, sectors), halo(8, -1, 1, 0, 3, sectors - 3, 3),
             halo(9, -1, -1, 0, 3, 0, 3)]

    def forward(k, q):
        return 1, remote(down.at[3 + far : 6 + far, q : q + 3], down.at[0:3, q : q + 3], down_sem, k, 1, 0)

    corners = [forward(10, 0), forward(11, 3 + sectors)]

    def start(copies):
        for dp, copy in copies:
            when(dp, copy.start)

    def arrive(copies):
        for dp, copy in copies:
            when(-dp, copy.wait_recv)

    lax.fori_loop(1, bands, later_band, 0)
    start(east)

    last_col.wait_recv()
    for h in range(halves):
        lanes = slice(h * LANES, (h + 1) * LANES)
        from_west = sum(
            west[h, pl.ds(8 * STEP // 4 - 1 + a, rows - STEP, stride=2), :] * w_depth[a, 0:1, lanes]
            for a in range(3))
        late[h, pl.ds(STEP * STEP, rows - STEP, stride=STEP), :] = from_west
    for p in range(1, bands):
        extra = jnp.concatenate(
            [late[h, STEP * STEP * p : STEP * STEP * (p + 1), :] for h in range(halves)], axis=1)
        down[3 + p, 3] = ((open_block[p] + extra) * open_sea[p]).astype(down.dtype)

    start(west_side + south)

    def from_north():
        last_row.wait_recv()
        last_cell.wait_recv()
        for h in range(halves):
            grid[h, 0, 7:8, :] = corner[h, 7:8, :]

    for h in range(halves):
        for r in range(2 * STEP):
            grid[h, 1 + r, 7:8, :] = west[h, r : r + 1, :]
    pl.when(has[-1])(from_north)
    block, sea = down_band(0)
    down[3, 3] = (block * sea).astype(down.dtype)

    start(top + north)

    def first(p, count, q, wide):
        flat = count * wide * STEP * STEP
        pieces = [
            down[p + a : p + a + count, q + b : q + b + wide].reshape(flat, chans)
            for a in range(3) for b in range(3)
        ]
        total = lax.dot_general(
            jnp.concatenate(pieces, axis=1),
            jnp.concatenate([one[a, b] for a in range(3) for b in range(3)], axis=1),
            (((1,), (1,)), ((), ())), preferred_element_type=jnp.float32)
        value = gelu(total + b_one[...].reshape(1, feats)).astype(hidden.dtype)
        hidden[p : p + count, q : q + wide, :, 0:feats] = value.reshape(
            count, wide, STEP * STEP, feats)

    load_one.wait()
    first(3, bands - 2, 3, sectors - 2)
    arrive(east[:1] + west_side[:1])
    start(corners)
    load_two.wait()
    if tail:
        for t in range(9):
            two_tail[t] = jnp.zeros(two_tail.shape[1:], two_tail.dtype)
            two_tail[t, 0:tail, :] = two[t // 3, t % 3, main:feats, :]
    arrive(east[1:] + top[:1])
    first(3, bands - 2, 0, 3)
    arrive(west_side[1:] + top[1:])
    first(3, bands - 2, sectors + 1, 3)
    arrive(south + corners)
    first(0, 3, 0, sectors + 4)

    def no_cells(lat_at, p):
        def body():
            hidden[p : p + 2] = jnp.zeros((2,) + hidden.shape[1:], hidden.dtype)

        pl.when(lat == lat_at)(body)

    no_cells(0, 0)

    def taps_of(buffer, places, taps, size):
        count = size[0] * size[1] * STEP * STEP
        window = [
            buffer[pl.ds(p, size[0]), q : q + size[1]].reshape(count, buffer.shape[3])
            for p, q in places
        ]
        total = jnp.dot(
            jnp.concatenate([cells[:, 0:main] for cells in window], axis=1),
            jnp.concatenate([two[a, b, 0:main, :] for a, b in taps], axis=0),
            preferred_element_type=jnp.float32)
        if tail:
            total = total + jnp.dot(
                jnp.concatenate([cells[:, main:] for cells in window], axis=1),
                jnp.concatenate([two_tail[3 * a + b] for a, b in taps], axis=0),
                preferred_element_type=jnp.float32)
        return total.reshape(size + (STEP * STEP, feats))

    every = [(a, b) for a in range(3) for b in range(3)]
    chunk = bands // 2

    def second(c):
        p = c * chunk
        sums[p : p + chunk] = taps_of(
            hidden, [(p + 2 * a, 2 * b) for a, b in every], every, (chunk, sectors))

    second(0)
    arrive(north)
    first(bands + 1, 3, 0, sectors + 4)
    no_cells(n_lat - 1, bands + 2)
    second(1)

    def finish(p, carry):
        value = gelu(sums[p] + b_two[...].reshape(1, 1, feats))
        for r in range(STEP):
            i = STEP * p + r
            out[i] = gather([value[q, STEP * r : STEP * r + STEP] for q in range(sectors)], 0) * mask[i][:, :feats]
        return carry

    lax.fori_loop(0, bands, finish, 0)

    last_col.wait_send()
    for dp, copy in [(1, last_row), (1, last_cell)] + east + west_side + south + top + north + corners:
        when(dp, copy.wait_send)


def on_device(n_lat, n_lon, fields, land_sea, w_depth, b_depth, w_one, b_one, w_two, b_two):
    rows, cols = land_sea.shape
    chans, feats = w_one.shape[2:]
    bands, sectors = rows // STEP, cols // STEP
    main = feats // (2 * LANES) * (2 * LANES)
    wide = up_to(feats, LANES)
    halves = chans // LANES
    taps_out_in = jnp.swapaxes(w_one, 2, 3)
    any_space = pl.BlockSpec(memory_space=pltpu.HBM)
    vmem = pl.BlockSpec(memory_space=pltpu.VMEM)
    return pl.pallas_call(
        functools.partial(kernel, (n_lat, n_lon, rows, cols, chans, feats)),
        out_shape=pltpu.VMEM((rows, cols, feats), jnp.float32),
        in_specs=[any_space, vmem, vmem, vmem, any_space, vmem, any_space, vmem],
        out_specs=vmem,
        scratch_shapes=[
            pltpu.VMEM((halves, 2 * rows + 1, 2 * cols + 8, LANES), jnp.float32),
            pltpu.VMEM((halves, 2 * rows, LANES), jnp.float32),
            pltpu.VMEM((halves, 2 * rows, LANES), jnp.float32),
            pltpu.VMEM((halves, 8, LANES), jnp.float32),
            pltpu.VMEM((halves, STEP * rows, LANES), jnp.float32),
            pltpu.VMEM((bands, STEP * STEP, chans), jnp.float32),
            pltpu.VMEM((bands, STEP * STEP, chans), jnp.float32),
            pltpu.VMEM((rows, cols, wide), jnp.float32),
            pltpu.VMEM((bands + 6, sectors + 6, STEP * STEP, chans), jnp.bfloat16),
            pltpu.VMEM((bands + 4, sectors + 4, STEP * STEP, wide), jnp.bfloat16),
            pltpu.VMEM(taps_out_in.shape, jnp.bfloat16),
            pltpu.VMEM(w_two.shape, jnp.bfloat16),
            pltpu.VMEM((9, max(wide - main, LANES), feats), jnp.bfloat16),
            pltpu.VMEM((bands, sectors, STEP * STEP, feats), jnp.float32),
            pltpu.SemaphoreType.DMA((2 + 2 * halves,)),
            pltpu.SemaphoreType.DMA((2, 3)),
            pltpu.SemaphoreType.DMA((2, 12)),
        ],
        compiler_params=pltpu.CompilerParams(
            collective_id=0, has_side_effects=True, vmem_limit_bytes=62 * 1024 * 1024),
    )(fields, land_sea.T, w_depth, b_depth, taps_out_in, b_one, w_two, b_two)


def solution(mesh):
    return jax.shard_map(
        functools.partial(on_device, mesh.shape["lat"], mesh.shape["lon"]),
        mesh=mesh,
        in_specs=(P("lat", "lon", None), P("lat", "lon"), P(), P(), P(), P(), P(), P()),
        out_specs=P("lat", "lon", None),
        check_vma=False,
    )
```

```python
import functools

import jax
import jax.numpy as jnp
from jax import lax
from jax.experimental import pallas as pl
from jax.experimental.pallas import tpu as pltpu
from jax.sharding import PartitionSpec as P

MESH = pl.DeviceIdType.MESH
SIDES = tuple((dp, dq) for dp in (-1, 0, 1) for dq in (-1, 0, 1) if (dp, dq) != (0, 0))
STEP = 4
LANES = 128


def gelu(x):
    return 0.5 * x * (1.0 + lax.erf(x * 0.7071067811865476))


def up_to(value, multiple):
    return -(-value // multiple) * multiple


def kernel(
    shape, fields, land, w_depth, b_depth, w_one, b_one, w_two, b_two, out,
    grid, edge, west, corner, late, open_block, open_sea, mask, down, hidden, one, one_in_out, two, two_tail, sums,
    load_sem, edge_sem, down_sem,
):
    n_lat, n_lon, rows, cols, chans, feats = shape
    bands, sectors = rows // STEP, cols // STEP
    main = feats // (2 * LANES) * (2 * LANES)
    tail = feats - main
    lat, lon = lax.axis_index("lat"), lax.axis_index("lon")
    has = {-1: lat > 0, 0: True, 1: lat < n_lat - 1}

    def when(dp, body):
        if dp == 0:
            body()
        else:
            pl.when(has[dp])(body)

    def device(dp, dq):
        return (lat + dp, lax.rem(lon + dq + n_lon, n_lon))

    halves = chans // LANES
    split = 2 * cols - 8

    def part(h, k):
        start, size = ((split, 8), (0, split))[k]
        return pltpu.make_async_copy(
            fields.at[:, start : start + size, h * LANES : (h + 1) * LANES],
            grid.at[h, 1:, 8 + start : 8 + start + size, :], load_sem.at[2 + 2 * h + k])

    edge_parts = [part(h, 0) for h in range(halves)]
    inner_parts = [part(h, 1) for h in range(halves)]
    load_one = pltpu.make_async_copy(w_one, one, load_sem.at[0])
    load_two = pltpu.make_async_copy(w_two, two, load_sem.at[1])
    for load in edge_parts + inner_parts:
        load.start()

    barrier = pltpu.get_barrier_semaphore()
    for dp, dq in SIDES:
        when(dp, lambda dp=dp, dq=dq: pl.semaphore_signal(
            barrier, inc=1, device_id=device(dp, dq), device_id_type=MESH))

    cells = land[...].astype(jnp.float32)
    for i in range(rows):
        mask[i] = jnp.broadcast_to(cells[:, i : i + 1], mask.shape[1:])

    for p in range(bands + 4):
        hidden[p] = jnp.zeros(hidden.shape[1:], hidden.dtype)

    def clear(buffer, width):
        gap = jnp.zeros((width,) + buffer.shape[1:], buffer.dtype)

        def north():
            buffer[0:width] = gap

        def south():
            buffer[buffer.shape[0] - width :] = gap

        pl.when(lat == 0)(north)
        pl.when(lat == n_lat - 1)(south)

    def no_north():
        grid[:, 0, 8:, :] = jnp.zeros((halves, 2 * cols, LANES), grid.dtype)

    pl.when(lat == 0)(no_north)
    clear(down, 3)

    for h in range(halves):
        edge_parts[h].wait()
        for r in range(2 * rows):
            edge[h, r : r + 1, :] = grid[h, 1 + r, 8 + 2 * cols - 1 : 8 + 2 * cols, :]

    pl.semaphore_wait(barrier, 2 + 3 * jnp.minimum(lat, 1) + 3 * jnp.minimum(n_lat - 1 - lat, 1))

    def remote(src, dst, sems, k, dp, dq):
        return pltpu.make_async_remote_copy(
            src_ref=src, dst_ref=dst, send_sem=sems.at[0, k], recv_sem=sems.at[1, k],
            device_id=device(dp, dq), device_id_type=MESH)

    last_row = remote(grid.at[:, 2 * rows, 8:, :], grid.at[:, 0, 8:, :], edge_sem, 0, 1, 0)
    last_col = remote(edge, west, edge_sem, 1, 0, 1)
    last_cell = remote(edge.at[:, 2 * rows - 8 :], corner, edge_sem, 2, 1, 1)
    last_col.start()
    when(1, last_cell.start)
    for inner in inner_parts:
        inner.wait()
    when(1, last_row.start)
    load_one.start()
    load_two.start()

    for h in range(halves):
        grid[h, :, 0:8, :] = jnp.zeros((2 * rows + 1, 8, LANES), grid.dtype)
        late[h] = jnp.zeros(late.shape[1:], late.dtype)

    def down_line(i):
        line = []
        for h in range(halves):
            lanes = slice(h * LANES, (h + 1) * LANES)
            total = jnp.broadcast_to(b_depth[...].reshape(1, chans)[:, lanes], (cols, LANES))
            for a in range(3):
                for b in range(3):
                    piece = grid[h, 2 * i + a, pl.ds(7 + b, cols, stride=2), :]
                    total = total + piece * w_depth[a, b : b + 1, lanes]
            line.append(total)
        return jnp.concatenate(line, axis=1)

    def gather(lines, q):
        return jnp.concatenate([line[STEP * q : STEP * q + STEP] for line in lines], axis=0)

    def down_band(p):
        lines = [down_line(STEP * p + r) for r in range(STEP)]
        seas = [mask[STEP * p + r][:, :chans] for r in range(STEP)]
        masked = [line * sea for line, sea in zip(lines, seas)]
        for q in range(1, sectors):
            down[3 + p, 3 + q] = gather(masked, q).astype(down.dtype)
        return gather(lines, 0), gather(seas, 0)

    def later_band(p, carry):
        block, sea = down_band(p)
        open_block[p] = block
        open_sea[p] = sea
        return carry

    def halo(k, dp, dq, p, count, q, wide):
        src = down.at[3 + p : 3 + p + count, 3 + q : 3 + q + wide]
        to_p, to_q = 3 + p - dp * bands, 3 + q - dq * sectors
        dst = down.at[to_p : to_p + count, to_q : to_q + wide]
        return dp, remote(src, dst, down_sem, k, dp, dq)

    far, last = bands - 3, sectors - 3
    east = [halo(0, 0, 1, far, 3, last, 3), halo(1, 0, 1, 1, far - 1, last, 3)]
    west_side = [halo(2, 0, -1, far, 3, 1, 2), halo(3, 0, -1, 1, far - 1, 1, 2)]
    south = [halo(4, 1, 0, far, 3, 1, sectors - 1)]
    north = [halo(5, -1, 0, 1, 2, 1, sectors - 1), halo(6, -1, 1, 1, 2, last, 3),
             halo(7, -1, -1, 1, 2, 1, 2)]
    west_late = [halo(8, 0, -1, far, 3, 0, 1), halo(9, 0, -1, 0, far, 0, 1)]
    south_late = [halo(10, 1, 0, far, 3, 0, 1)]
    top = [halo(11, 0, 1, 0, 1, last, 3), halo(12, 0, -1, 0, 1, 1, 2)]
    north_late = [halo(13, -1, 0, 0, 1, 0, sectors), halo(14, -1, 0, 1, 2, 0, 1),
                  halo(15, -1, 1, 0, 1, last, 3),
                  halo(16, -1, -1, 0, 1, 0, 3), halo(17, -1, -1, 1, 2, 0, 1)]

    def forward(k, q, wide):
        return 1, remote(
            down.at[3 + far : 6 + far, q : q + wide], down.at[0:3, q : q + wide], down_sem, k, 1, 0)

    corners = [forward(18, 0, 3), forward(19, 4 + sectors, 2), forward(20, 3 + sectors, 1)]

    def start(copies):
        for dp, copy in copies:
            when(dp, copy.start)

    def arrive(copies):
        for dp, copy in copies:
            when(-dp, copy.wait_recv)

    lax.fori_loop(1, bands, later_band, 0)
    start(east[:1] + west_side[:1] + north[1:] + east[1:] + west_side[1:] + south + north[:1])

    last_col.wait_recv()
    for h in range(halves):
        lanes = slice(h * LANES, (h + 1) * LANES)
        from_west = sum(
            west[h, pl.ds(8 * STEP // 4 - 1 + a, rows - STEP, stride=2), :] * w_depth[a, 0:1, lanes]
            for a in range(3))
        late[h, pl.ds(STEP * STEP, rows - STEP, stride=STEP), :] = from_west
    for p in range(1, bands):
        extra = jnp.concatenate(
            [late[h, STEP * STEP * p : STEP * STEP * (p + 1), :] for h in range(halves)], axis=1)
        down[3 + p, 3] = ((open_block[p] + extra) * open_sea[p]).astype(down.dtype)

    def from_north():
        last_row.wait_recv()
        last_cell.wait_recv()
        for h in range(halves):
            grid[h, 0, 7:8, :] = corner[h, 7:8, :]

    for h in range(halves):
        for r in range(2 * STEP):
            grid[h, 1 + r, 7:8, :] = west[h, r : r + 1, :]
    pl.when(has[-1])(from_north)
    block, sea = down_band(0)
    down[3, 3] = (block * sea).astype(down.dtype)

    start(west_late + north_late[2:] + top + south_late + north_late[:2])

    def first(p, count, q, wide):
        flat = count * wide * STEP * STEP
        pieces = [
            down[p + a : p + a + count, q + b : q + b + wide].reshape(flat, chans)
            for a in range(3) for b in range(3)
        ]
        total = jnp.dot(
            jnp.concatenate(pieces, axis=1), one_in_out[...].reshape(9 * chans, feats),
            preferred_element_type=jnp.float32)
        value = gelu(total + b_one[...].reshape(1, feats)).astype(hidden.dtype)
        hidden[p : p + count, q : q + wide, :, 0:feats] = value.reshape(
            count, wide, STEP * STEP, feats)

    load_one.wait()

    def turn(t, carry):
        tap = one.at[t // 3, lax.rem(t, 3)]
        one_in_out[t, :, 0:main] = jnp.transpose(tap[0:main, :])
        if tail:
            rest = jnp.concatenate(
                [tap[main:feats, :], jnp.zeros((up_to(tail, LANES) - tail, chans), one.dtype)], axis=0)
            one_in_out[t, :, main:feats] = jnp.transpose(rest)[:, 0:tail]
        return carry

    lax.fori_loop(0, 9, turn, 0)
    arrive(east[:1] + west_side[:1])
    start(corners[:2])
    first(3, bands - 2, 3, sectors - 2)
    arrive(west_late[:1])
    start(corners[2:])
    load_two.wait()
    if tail:
        for t in range(9):
            two_tail[t] = jnp.zeros(two_tail.shape[1:], two_tail.dtype)
            two_tail[t, 0:tail, :] = two[t // 3, t % 3, main:feats, :]
    arrive(east[1:] + top[:1])
    first(3, bands - 2, 0, 3)
    arrive(west_side[1:] + west_late[1:] + top[1:])
    first(3, bands - 2, sectors + 1, 3)
    arrive(south + south_late + corners)
    first(0, 3, 0, sectors + 4)

    def no_cells(lat_at, p):
        def body():
            hidden[p : p + 2] = jnp.zeros((2,) + hidden.shape[1:], hidden.dtype)

        pl.when(lat == lat_at)(body)

    no_cells(0, 0)

    def taps_of(buffer, places, taps, size):
        count = size[0] * size[1] * STEP * STEP
        window = [
            buffer[pl.ds(p, size[0]), q : q + size[1]].reshape(count, buffer.shape[3])
            for p, q in places
        ]
        total = jnp.dot(
            jnp.concatenate([cells[:, 0:main] for cells in window], axis=1),
            jnp.concatenate([two[a, b, 0:main, :] for a, b in taps], axis=0),
            preferred_element_type=jnp.float32)
        if tail:
            total = total + jnp.dot(
                jnp.concatenate([cells[:, main:] for cells in window], axis=1),
                jnp.concatenate([two_tail[3 * a + b] for a, b in taps], axis=0),
                preferred_element_type=jnp.float32)
        return total.reshape(size + (STEP * STEP, feats))

    every = [(a, b) for a in range(3) for b in range(3)]
    chunk = bands // 2

    def second(c):
        p = c * chunk
        sums[p : p + chunk] = taps_of(
            hidden, [(p + 2 * a, 2 * b) for a, b in every], every, (chunk, sectors))

    second(0)
    arrive(north + north_late)
    first(bands + 1, 3, 0, sectors + 4)
    no_cells(n_lat - 1, bands + 2)
    second(1)

    def finish(p, carry):
        value = gelu(sums[p] + b_two[...].reshape(1, 1, feats))
        for r in range(STEP):
            i = STEP * p + r
            out[i] = gather([value[q, STEP * r : STEP * r + STEP] for q in range(sectors)], 0) * mask[i][:, :feats]
        return carry

    lax.fori_loop(0, bands, finish, 0)

    last_col.wait_send()
    for dp, copy in [(1, last_row), (1, last_cell)] + (
            east + west_side + south + north + west_late + south_late + top + north_late + corners):
        when(dp, copy.wait_send)


def on_device(n_lat, n_lon, fields, land_sea, w_depth, b_depth, w_one, b_one, w_two, b_two):
    rows, cols = land_sea.shape
    chans, feats = w_one.shape[2:]
    bands, sectors = rows // STEP, cols // STEP
    main = feats // (2 * LANES) * (2 * LANES)
    wide = up_to(feats, LANES)
    halves = chans // LANES
    taps_out_in = jnp.swapaxes(w_one, 2, 3)
    any_space = pl.BlockSpec(memory_space=pltpu.HBM)
    vmem = pl.BlockSpec(memory_space=pltpu.VMEM)
    return pl.pallas_call(
        functools.partial(kernel, (n_lat, n_lon, rows, cols, chans, feats)),
        out_shape=pltpu.VMEM((rows, cols, feats), jnp.float32),
        in_specs=[any_space, vmem, vmem, vmem, any_space, vmem, any_space, vmem],
        out_specs=vmem,
        scratch_shapes=[
            pltpu.VMEM((halves, 2 * rows + 1, 2 * cols + 8, LANES), jnp.float32),
            pltpu.VMEM((halves, 2 * rows, LANES), jnp.float32),
            pltpu.VMEM((halves, 2 * rows, LANES), jnp.float32),
            pltpu.VMEM((halves, 8, LANES), jnp.float32),
            pltpu.VMEM((halves, STEP * rows, LANES), jnp.float32),
            pltpu.VMEM((bands, STEP * STEP, chans), jnp.float32),
            pltpu.VMEM((bands, STEP * STEP, chans), jnp.float32),
            pltpu.VMEM((rows, cols, wide), jnp.float32),
            pltpu.VMEM((bands + 6, sectors + 6, STEP * STEP, chans), jnp.bfloat16),
            pltpu.VMEM((bands + 4, sectors + 4, STEP * STEP, wide), jnp.bfloat16),
            pltpu.VMEM(taps_out_in.shape, jnp.bfloat16),
            pltpu.VMEM((9, chans, feats), jnp.bfloat16),
            pltpu.VMEM(w_two.shape, jnp.bfloat16),
            pltpu.VMEM((9, max(wide - main, LANES), feats), jnp.bfloat16),
            pltpu.VMEM((bands, sectors, STEP * STEP, feats), jnp.float32),
            pltpu.SemaphoreType.DMA((2 + 2 * halves,)),
            pltpu.SemaphoreType.DMA((2, 3)),
            pltpu.SemaphoreType.DMA((2, 21)),
        ],
        compiler_params=pltpu.CompilerParams(
            collective_id=0, has_side_effects=True, vmem_limit_bytes=62 * 1024 * 1024),
    )(fields, land_sea.T, w_depth, b_depth, taps_out_in, b_one, w_two, b_two)


def solution(mesh):
    return jax.shard_map(
        functools.partial(on_device, mesh.shape["lat"], mesh.shape["lon"]),
        mesh=mesh,
        in_specs=(P("lat", "lon", None), P("lat", "lon"), P(), P(), P(), P(), P(), P()),
        out_specs=P("lat", "lon", None),
        check_vma=False,
    )
```

```python
import functools

import jax
import jax.numpy as jnp
from jax import lax
from jax.experimental import pallas as pl
from jax.experimental.pallas import tpu as pltpu
from jax.sharding import PartitionSpec as P

MESH = pl.DeviceIdType.MESH
SIDES = tuple((dp, dq) for dp in (-1, 0, 1) for dq in (-1, 0, 1) if (dp, dq) != (0, 0))
STEP = 4
LANES = 128


def gelu(x):
    return 0.5 * x * (1.0 + lax.erf(x * 0.7071067811865476))


def up_to(value, multiple):
    return -(-value // multiple) * multiple


def kernel(
    shape, fields, land, w_depth, b_depth, w_one, b_one, w_two, b_two, out,
    grid, edge, west, corner, late, open_block, open_sea, mask, down, hidden, one, two, two_tail, sums,
    load_sem, edge_sem, down_sem,
):
    n_lat, n_lon, rows, cols, chans, feats = shape
    bands, sectors = rows // STEP, cols // STEP
    main = feats // (2 * LANES) * (2 * LANES)
    tail = feats - main
    lat, lon = lax.axis_index("lat"), lax.axis_index("lon")
    has = {-1: lat > 0, 0: True, 1: lat < n_lat - 1}

    def when(dp, body):
        if dp == 0:
            body()
        else:
            pl.when(has[dp])(body)

    def device(dp, dq):
        return (lat + dp, lax.rem(lon + dq + n_lon, n_lon))

    halves = chans // LANES
    split = 2 * cols - 8

    def part(h, k):
        start, size = ((split, 8), (0, split))[k]
        return pltpu.make_async_copy(
            fields.at[:, start : start + size, h * LANES : (h + 1) * LANES],
            grid.at[h, 1:, 8 + start : 8 + start + size, :], load_sem.at[2 + 2 * h + k])

    edge_parts = [part(h, 0) for h in range(halves)]
    inner_parts = [part(h, 1) for h in range(halves)]
    load_one = pltpu.make_async_copy(w_one, one, load_sem.at[0])
    load_two = pltpu.make_async_copy(w_two, two, load_sem.at[1])
    for load in edge_parts + inner_parts:
        load.start()

    barrier = pltpu.get_barrier_semaphore()
    for dp, dq in SIDES:
        when(dp, lambda dp=dp, dq=dq: pl.semaphore_signal(
            barrier, inc=1, device_id=device(dp, dq), device_id_type=MESH))

    cells = land[...].astype(jnp.float32)
    for i in range(rows):
        mask[i] = jnp.broadcast_to(cells[:, i : i + 1], mask.shape[1:])

    if tail:
        for p in range(bands + 4):
            hidden[p, :, :, main:] = jnp.zeros(hidden.shape[1:3] + (hidden.shape[3] - main,), hidden.dtype)

    def clear(buffer, width):
        gap = jnp.zeros((width,) + buffer.shape[1:], buffer.dtype)

        def north():
            buffer[0:width] = gap

        def south():
            buffer[buffer.shape[0] - width :] = gap

        pl.when(lat == 0)(north)
        pl.when(lat == n_lat - 1)(south)

    def no_north():
        grid[:, 0, 8:, :] = jnp.zeros((halves, 2 * cols, LANES), grid.dtype)

    pl.when(lat == 0)(no_north)
    clear(down, 3)

    for h in range(halves):
        edge_parts[h].wait()
        for r in range(2 * rows):
            edge[h, r : r + 1, :] = grid[h, 1 + r, 8 + 2 * cols - 1 : 8 + 2 * cols, :]

    pl.semaphore_wait(barrier, 2 + 3 * jnp.minimum(lat, 1) + 3 * jnp.minimum(n_lat - 1 - lat, 1))

    def remote(src, dst, sems, k, dp, dq):
        return pltpu.make_async_remote_copy(
            src_ref=src, dst_ref=dst, send_sem=sems.at[0, k], recv_sem=sems.at[1, k],
            device_id=device(dp, dq), device_id_type=MESH)

    last_row = remote(grid.at[:, 2 * rows, 8:, :], grid.at[:, 0, 8:, :], edge_sem, 0, 1, 0)
    last_col = remote(edge, west, edge_sem, 1, 0, 1)
    last_cell = remote(edge.at[:, 2 * rows - 8 :], corner, edge_sem, 2, 1, 1)
    last_col.start()
    when(1, last_cell.start)
    for inner in inner_parts:
        inner.wait()
    when(1, last_row.start)
    load_one.start()
    load_two.start()

    for h in range(halves):
        grid[h, :, 0:8, :] = jnp.zeros((2 * rows + 1, 8, LANES), grid.dtype)
        late[h] = jnp.zeros(late.shape[1:], late.dtype)

    def down_line(i):
        line = []
        for h in range(halves):
            lanes = slice(h * LANES, (h + 1) * LANES)
            total = jnp.broadcast_to(b_depth[...].reshape(1, chans)[:, lanes], (cols, LANES))
            for a in range(3):
                for b in range(3):
                    piece = grid[h, 2 * i + a, pl.ds(7 + b, cols, stride=2), :]
                    total = total + piece * w_depth[a, b : b + 1, lanes]
            line.append(total)
        return jnp.concatenate(line, axis=1)

    def gather(lines, q):
        return jnp.concatenate([line[STEP * q : STEP * q + STEP] for line in lines], axis=0)

    def down_band(p):
        lines = [down_line(STEP * p + r) for r in range(STEP)]
        seas = [mask[STEP * p + r][:, :chans] for r in range(STEP)]
        masked = [line * sea for line, sea in zip(lines, seas)]
        for q in range(1, sectors):
            down[3 + p, 3 + q] = gather(masked, q).astype(down.dtype)
        return gather(lines, 0), gather(seas, 0)

    def later_band(p, carry):
        block, sea = down_band(p)
        open_block[p] = block
        open_sea[p] = sea
        return carry

    def halo(k, dp, dq, p, count, q, wide):
        src = down.at[3 + p : 3 + p + count, 3 + q : 3 + q + wide]
        to_p, to_q = 3 + p - dp * bands, 3 + q - dq * sectors
        dst = down.at[to_p : to_p + count, to_q : to_q + wide]
        return dp, remote(src, dst, down_sem, k, dp, dq)

    far, last = bands - 3, sectors - 3
    east = [halo(0, 0, 1, far, 3, last, 3), halo(1, 0, 1, 1, far - 1, last, 3)]
    west_side = [halo(2, 0, -1, far, 3, 1, 2), halo(3, 0, -1, 1, far - 1, 1, 2)]
    south = [halo(4, 1, 0, far, 3, 1, sectors - 1)]
    north = [halo(5, -1, 0, 1, 2, 1, sectors - 1), halo(6, -1, 1, 1, 2, last, 3),
             halo(7, -1, -1, 1, 2, 1, 2)]
    west_late = [halo(8, 0, -1, far, 3, 0, 1), halo(9, 0, -1, 0, far, 0, 1)]
    south_late = [halo(10, 1, 0, far, 3, 0, 1)]
    top = [halo(11, 0, 1, 0, 1, last, 3), halo(12, 0, -1, 0, 1, 1, 2)]
    north_late = [halo(13, -1, 0, 0, 1, 0, sectors), halo(14, -1, 0, 1, 2, 0, 1),
                  halo(15, -1, 1, 0, 1, last, 3),
                  halo(16, -1, -1, 0, 1, 0, 3), halo(17, -1, -1, 1, 2, 0, 1)]

    def forward(k, q, wide):
        return 1, remote(
            down.at[3 + far : 6 + far, q : q + wide], down.at[0:3, q : q + wide], down_sem, k, 1, 0)

    corners = [forward(18, 0, 3), forward(19, 3 + sectors, 3)]

    def start(copies):
        for dp, copy in copies:
            when(dp, copy.start)

    def arrive(copies):
        for dp, copy in copies:
            when(-dp, copy.wait_recv)

    lax.fori_loop(1, bands, later_band, 0)
    start(east[:1] + west_side[:1] + north[1:] + east[1:] + west_side[1:] + south + north[:1])

    last_col.wait_recv()
    for h in range(halves):
        lanes = slice(h * LANES, (h + 1) * LANES)
        from_west = sum(
            west[h, pl.ds(8 * STEP // 4 - 1 + a, rows - STEP, stride=2), :] * w_depth[a, 0:1, lanes]
            for a in range(3))
        late[h, pl.ds(STEP * STEP, rows - STEP, stride=STEP), :] = from_west
    for p in range(1, bands):
        extra = jnp.concatenate(
            [late[h, STEP * STEP * p : STEP * STEP * (p + 1), :] for h in range(halves)], axis=1)
        down[3 + p, 3] = ((open_block[p] + extra) * open_sea[p]).astype(down.dtype)

    def from_north():
        last_row.wait_recv()
        last_cell.wait_recv()
        for h in range(halves):
            grid[h, 0, 7:8, :] = corner[h, 7:8, :]

    for h in range(halves):
        for r in range(2 * STEP):
            grid[h, 1 + r, 7:8, :] = west[h, r : r + 1, :]
    pl.when(has[-1])(from_north)
    block, sea = down_band(0)
    down[3, 3] = (block * sea).astype(down.dtype)

    start(west_late + north_late[2:] + top + south_late + north_late[:2])

    def first(p, count, q, wide):
        flat = count * wide * STEP * STEP
        pieces = [
            down[p + a : p + a + count, q + b : q + b + wide].reshape(flat, chans)
            for a in range(3) for b in range(3)
        ]
        total = lax.dot_general(
            jnp.concatenate(pieces, axis=1),
            jnp.concatenate([one[a, b] for a in range(3) for b in range(3)], axis=1),
            (((1,), (1,)), ((), ())), preferred_element_type=jnp.float32)
        value = gelu(total + b_one[...].reshape(1, feats)).astype(hidden.dtype)
        hidden[p : p + count, q : q + wide, :, 0:feats] = value.reshape(
            count, wide, STEP * STEP, feats)

    load_one.wait()
    first(3, bands - 2, 3, sectors - 2)
    arrive(east[:1] + west_side[:1] + west_late[:1])
    start(corners)
    load_two.wait()
    if tail:
        for t in range(9):
            two_tail[t] = jnp.zeros(two_tail.shape[1:], two_tail.dtype)
            two_tail[t, 0:tail, :] = two[t // 3, t % 3, main:feats, :]
    arrive(east[1:] + top[:1])
    first(3, bands - 2, 0, 3)
    arrive(west_side[1:] + west_late[1:] + top[1:])
    first(3, bands - 2, sectors + 1, 3)
    arrive(south + south_late + corners)
    first(0, 3, 0, sectors + 4)

    def no_cells(lat_at, p):
        def body():
            hidden[p : p + 2] = jnp.zeros((2,) + hidden.shape[1:], hidden.dtype)

        pl.when(lat == lat_at)(body)

    no_cells(0, 0)

    def taps_of(buffer, places, taps, size):
        count = size[0] * size[1] * STEP * STEP
        window = [
            buffer[pl.ds(p, size[0]), q : q + size[1]].reshape(count, buffer.shape[3])
            for p, q in places
        ]
        total = jnp.dot(
            jnp.concatenate([cells[:, 0:main] for cells in window], axis=1),
            jnp.concatenate([two[a, b, 0:main, :] for a, b in taps], axis=0),
            preferred_element_type=jnp.float32)
        if tail:
            total = total + jnp.dot(
                jnp.concatenate([cells[:, main:] for cells in window], axis=1),
                jnp.concatenate([two_tail[3 * a + b] for a, b in taps], axis=0),
                preferred_element_type=jnp.float32)
        return total.reshape(size + (STEP * STEP, feats))

    every = [(a, b) for a in range(3) for b in range(3)]
    chunk = bands // 2

    def second(c):
        p = c * chunk
        sums[p : p + chunk] = taps_of(
            hidden, [(p + 2 * a, 2 * b) for a, b in every], every, (chunk, sectors))

    second(0)
    arrive(north + north_late)
    first(bands + 1, 3, 0, sectors + 4)
    no_cells(n_lat - 1, bands + 2)
    second(1)

    def finish(p, carry):
        value = gelu(sums[p] + b_two[...].reshape(1, 1, feats))
        for r in range(STEP):
            i = STEP * p + r
            out[i] = gather([value[q, STEP * r : STEP * r + STEP] for q in range(sectors)], 0) * mask[i][:, :feats]
        return carry

    lax.fori_loop(0, bands, finish, 0)

    last_col.wait_send()
    for dp, copy in [(1, last_row), (1, last_cell)] + (
            east + west_side + south + north + west_late + south_late + top + north_late + corners):
        when(dp, copy.wait_send)


def on_device(n_lat, n_lon, fields, land_sea, w_depth, b_depth, w_one, b_one, w_two, b_two):
    rows, cols = land_sea.shape
    chans, feats = w_one.shape[2:]
    bands, sectors = rows // STEP, cols // STEP
    main = feats // (2 * LANES) * (2 * LANES)
    wide = up_to(feats, LANES)
    halves = chans // LANES
    taps_out_in = jnp.swapaxes(w_one, 2, 3)
    any_space = pl.BlockSpec(memory_space=pltpu.HBM)
    vmem = pl.BlockSpec(memory_space=pltpu.VMEM)
    return pl.pallas_call(
        functools.partial(kernel, (n_lat, n_lon, rows, cols, chans, feats)),
        out_shape=pltpu.VMEM((rows, cols, feats), jnp.float32),
        in_specs=[any_space, vmem, vmem, vmem, any_space, vmem, any_space, vmem],
        out_specs=vmem,
        scratch_shapes=[
            pltpu.VMEM((halves, 2 * rows + 1, 2 * cols + 8, LANES), jnp.float32),
            pltpu.VMEM((halves, 2 * rows, LANES), jnp.float32),
            pltpu.VMEM((halves, 2 * rows, LANES), jnp.float32),
            pltpu.VMEM((halves, 8, LANES), jnp.float32),
            pltpu.VMEM((halves, STEP * rows, LANES), jnp.float32),
            pltpu.VMEM((bands, STEP * STEP, chans), jnp.float32),
            pltpu.VMEM((bands, STEP * STEP, chans), jnp.float32),
            pltpu.VMEM((rows, cols, wide), jnp.float32),
            pltpu.VMEM((bands + 6, sectors + 6, STEP * STEP, chans), jnp.bfloat16),
            pltpu.VMEM((bands + 4, sectors + 4, STEP * STEP, wide), jnp.bfloat16),
            pltpu.VMEM(taps_out_in.shape, jnp.bfloat16),
            pltpu.VMEM(w_two.shape, jnp.bfloat16),
            pltpu.VMEM((9, max(wide - main, LANES), feats), jnp.bfloat16),
            pltpu.VMEM((bands, sectors, STEP * STEP, feats), jnp.float32),
            pltpu.SemaphoreType.DMA((2 + 2 * halves,)),
            pltpu.SemaphoreType.DMA((2, 3)),
            pltpu.SemaphoreType.DMA((2, 20)),
        ],
        compiler_params=pltpu.CompilerParams(
            collective_id=0, has_side_effects=True, vmem_limit_bytes=62 * 1024 * 1024),
    )(fields, land_sea.T, w_depth, b_depth, taps_out_in, b_one, w_two, b_two)


def solution(mesh):
    return jax.shard_map(
        functools.partial(on_device, mesh.shape["lat"], mesh.shape["lon"]),
        mesh=mesh,
        in_specs=(P("lat", "lon", None), P("lat", "lon"), P(), P(), P(), P(), P(), P()),
        out_specs=P("lat", "lon", None),
        check_vma=False,
    )
```

```python
import functools

import jax
import jax.numpy as jnp
from jax import lax
from jax.experimental import pallas as pl
from jax.experimental.pallas import tpu as pltpu
from jax.sharding import PartitionSpec as P

MESH = pl.DeviceIdType.MESH
SIDES = tuple((dp, dq) for dp in (-1, 0, 1) for dq in (-1, 0, 1) if (dp, dq) != (0, 0))
STEP = 4
LANES = 128


def gelu(x):
    return 0.5 * x * (1.0 + lax.erf(x * 0.7071067811865476))


def up_to(value, multiple):
    return -(-value // multiple) * multiple


def kernel(
    shape, fields, land, w_depth, b_depth, w_one, b_one, w_two, b_two, out,
    grid, edge, west, corner, late, open_block, open_sea, mask, down, hidden, one, one_in_out, two, two_tail, sums,
    load_sem, edge_sem, down_sem,
):
    n_lat, n_lon, rows, cols, chans, feats = shape
    bands, sectors = rows // STEP, cols // STEP
    main = feats // (2 * LANES) * (2 * LANES)
    tail = feats - main
    lat, lon = lax.axis_index("lat"), lax.axis_index("lon")
    has = {-1: lat > 0, 0: True, 1: lat < n_lat - 1}

    def when(dp, body):
        if dp == 0:
            body()
        else:
            pl.when(has[dp])(body)

    def device(dp, dq):
        return (lat + dp, lax.rem(lon + dq + n_lon, n_lon))

    halves = chans // LANES
    split = 2 * cols - 8

    def part(h, k):
        start, size = ((split, 8), (0, split))[k]
        return pltpu.make_async_copy(
            fields.at[:, start : start + size, h * LANES : (h + 1) * LANES],
            grid.at[h, 1:, 8 + start : 8 + start + size, :], load_sem.at[2 + 2 * h + k])

    edge_parts = [part(h, 0) for h in range(halves)]
    inner_parts = [part(h, 1) for h in range(halves)]
    load_one = pltpu.make_async_copy(w_one, one, load_sem.at[0])
    load_two = pltpu.make_async_copy(w_two, two, load_sem.at[1])
    for load in edge_parts + inner_parts:
        load.start()

    barrier = pltpu.get_barrier_semaphore()
    for dp, dq in SIDES:
        when(dp, lambda dp=dp, dq=dq: pl.semaphore_signal(
            barrier, inc=1, device_id=device(dp, dq), device_id_type=MESH))

    cells = land[...].astype(jnp.float32)
    for i in range(rows):
        mask[i] = jnp.broadcast_to(cells[:, i : i + 1], mask.shape[1:])

    if tail:
        for p in range(bands + 4):
            hidden[p, :, :, main:] = jnp.zeros(hidden.shape[1:3] + (hidden.shape[3] - main,), hidden.dtype)

    def clear(buffer, width):
        gap = jnp.zeros((width,) + buffer.shape[1:], buffer.dtype)

        def north():
            buffer[0:width] = gap

        def south():
            buffer[buffer.shape[0] - width :] = gap

        pl.when(lat == 0)(north)
        pl.when(lat == n_lat - 1)(south)

    def no_north():
        grid[:, 0, 8:, :] = jnp.zeros((halves, 2 * cols, LANES), grid.dtype)

    pl.when(lat == 0)(no_north)
    clear(down, 3)

    for h in range(halves):
        edge_parts[h].wait()
        for r in range(2 * rows):
            edge[h, r : r + 1, :] = grid[h, 1 + r, 8 + 2 * cols - 1 : 8 + 2 * cols, :]

    pl.semaphore_wait(barrier, 2 + 3 * jnp.minimum(lat, 1) + 3 * jnp.minimum(n_lat - 1 - lat, 1))

    def remote(src, dst, sems, k, dp, dq):
        return pltpu.make_async_remote_copy(
            src_ref=src, dst_ref=dst, send_sem=sems.at[0, k], recv_sem=sems.at[1, k],
            device_id=device(dp, dq), device_id_type=MESH)

    last_row = remote(grid.at[:, 2 * rows, 8:, :], grid.at[:, 0, 8:, :], edge_sem, 0, 1, 0)
    last_col = remote(edge, west, edge_sem, 1, 0, 1)
    last_cell = remote(edge.at[:, 2 * rows - 8 :], corner, edge_sem, 2, 1, 1)
    last_col.start()
    when(1, last_cell.start)
    for inner in inner_parts:
        inner.wait()
    when(1, last_row.start)
    load_one.start()
    load_two.start()

    for h in range(halves):
        grid[h, :, 0:8, :] = jnp.zeros((2 * rows + 1, 8, LANES), grid.dtype)
        late[h] = jnp.zeros(late.shape[1:], late.dtype)

    def down_line(i):
        line = []
        for h in range(halves):
            lanes = slice(h * LANES, (h + 1) * LANES)
            total = jnp.broadcast_to(b_depth[...].reshape(1, chans)[:, lanes], (cols, LANES))
            for a in range(3):
                for b in range(3):
                    piece = grid[h, 2 * i + a, pl.ds(7 + b, cols, stride=2), :]
                    total = total + piece * w_depth[a, b : b + 1, lanes]
            line.append(total)
        return jnp.concatenate(line, axis=1)

    def gather(lines, q):
        return jnp.concatenate([line[STEP * q : STEP * q + STEP] for line in lines], axis=0)

    def down_band(p):
        lines = [down_line(STEP * p + r) for r in range(STEP)]
        seas = [mask[STEP * p + r][:, :chans] for r in range(STEP)]
        masked = [line * sea for line, sea in zip(lines, seas)]
        for q in range(1, sectors):
            down[3 + p, 3 + q] = gather(masked, q).astype(down.dtype)
        return gather(lines, 0), gather(seas, 0)

    def later_band(p, carry):
        block, sea = down_band(p)
        open_block[p] = block
        open_sea[p] = sea
        return carry

    def halo(k, dp, dq, p, count, q, wide):
        src = down.at[3 + p : 3 + p + count, 3 + q : 3 + q + wide]
        to_p, to_q = 3 + p - dp * bands, 3 + q - dq * sectors
        dst = down.at[to_p : to_p + count, to_q : to_q + wide]
        return dp, remote(src, dst, down_sem, k, dp, dq)

    far = bands - 3
    east = [halo(0, 0, 1, far, 3, sectors - 3, 3), halo(1, 0, 1, 1, far - 1, sectors - 3, 3)]
    west_side = [halo(2, 0, -1, far, 3, 0, 3), halo(3, 0, -1, 1, far - 1, 0, 3)]
    south = [halo(4, 1, 0, far, 3, 0, sectors)]
    top = [halo(5, 0, 1, 0, 1, sectors - 3, 3), halo(6, 0, -1, 0, 1, 0, 3)]
    north = [halo(7, -1, 0, 0, 3, 0, sectors), halo(8, -1, 1, 0, 3, sectors - 3, 3),
             halo(9, -1, -1, 0, 3, 0, 3)]

    def forward(k, q):
        return 1, remote(down.at[3 + far : 6 + far, q : q + 3], down.at[0:3, q : q + 3], down_sem, k, 1, 0)

    corners = [forward(10, 0), forward(11, 3 + sectors)]

    def start(copies):
        for dp, copy in copies:
            when(dp, copy.start)

    def arrive(copies):
        for dp, copy in copies:
            when(-dp, copy.wait_recv)

    lax.fori_loop(1, bands, later_band, 0)
    start(east)

    last_col.wait_recv()
    for h in range(halves):
        lanes = slice(h * LANES, (h + 1) * LANES)
        from_west = sum(
            west[h, pl.ds(8 * STEP // 4 - 1 + a, rows - STEP, stride=2), :] * w_depth[a, 0:1, lanes]
            for a in range(3))
        late[h, pl.ds(STEP * STEP, rows - STEP, stride=STEP), :] = from_west
    for p in range(1, bands):
        extra = jnp.concatenate(
            [late[h, STEP * STEP * p : STEP * STEP * (p + 1), :] for h in range(halves)], axis=1)
        down[3 + p, 3] = ((open_block[p] + extra) * open_sea[p]).astype(down.dtype)

    start(west_side + south)

    def from_north():
        last_row.wait_recv()
        last_cell.wait_recv()
        for h in range(halves):
            grid[h, 0, 7:8, :] = corner[h, 7:8, :]

    for h in range(halves):
        for r in range(2 * STEP):
            grid[h, 1 + r, 7:8, :] = west[h, r : r + 1, :]
    pl.when(has[-1])(from_north)
    block, sea = down_band(0)
    down[3, 3] = (block * sea).astype(down.dtype)

    start(top + north)

    def first(p, count, q, wide):
        flat = count * wide * STEP * STEP
        pieces = [
            down[p + a : p + a + count, q + b : q + b + wide].reshape(flat, chans)
            for a in range(3) for b in range(3)
        ]
        total = jnp.dot(
            jnp.concatenate(pieces, axis=1), one_in_out[...].reshape(9 * chans, feats),
            preferred_element_type=jnp.float32)
        value = gelu(total + b_one[...].reshape(1, feats)).astype(hidden.dtype)
        hidden[p : p + count, q : q + wide, :, 0:feats] = value.reshape(
            count, wide, STEP * STEP, feats)

    load_one.wait()

    def turn(t, carry):
        tap = one.at[t // 3, lax.rem(t, 3)]
        one_in_out[t, :, 0:main] = jnp.transpose(tap[0:main, :])
        if tail:
            rest = jnp.concatenate(
                [tap[main:feats, :], jnp.zeros((up_to(tail, LANES) - tail, chans), one.dtype)], axis=0)
            one_in_out[t, :, main:feats] = jnp.transpose(rest)[:, 0:tail]
        return carry

    lax.fori_loop(0, 9, turn, 0)
    first(3, bands - 2, 3, sectors - 2)
    arrive(east[:1] + west_side[:1])
    start(corners)
    load_two.wait()
    if tail:
        for t in range(9):
            two_tail[t] = jnp.zeros(two_tail.shape[1:], two_tail.dtype)
            two_tail[t, 0:tail, :] = two[t // 3, t % 3, main:feats, :]
    arrive(east[1:] + top[:1])
    first(3, bands - 2, 0, 3)
    arrive(west_side[1:] + top[1:])
    first(3, bands - 2, sectors + 1, 3)
    arrive(south + corners)
    first(0, 3, 0, sectors + 4)

    def no_cells(lat_at, p):
        def body():
            hidden[p : p + 2] = jnp.zeros((2,) + hidden.shape[1:], hidden.dtype)

        pl.when(lat == lat_at)(body)

    no_cells(0, 0)

    def taps_of(buffer, places, taps, size):
        count = size[0] * size[1] * STEP * STEP
        window = [
            buffer[pl.ds(p, size[0]), q : q + size[1]].reshape(count, buffer.shape[3])
            for p, q in places
        ]
        total = jnp.dot(
            jnp.concatenate([cells[:, 0:main] for cells in window], axis=1),
            jnp.concatenate([two[a, b, 0:main, :] for a, b in taps], axis=0),
            preferred_element_type=jnp.float32)
        if tail:
            total = total + jnp.dot(
                jnp.concatenate([cells[:, main:] for cells in window], axis=1),
                jnp.concatenate([two_tail[3 * a + b] for a, b in taps], axis=0),
                preferred_element_type=jnp.float32)
        return total.reshape(size + (STEP * STEP, feats))

    every = [(a, b) for a in range(3) for b in range(3)]
    early = bands - 3

    def second(p, count):
        sums[p : p + count] = taps_of(
            hidden, [(p + 2 * a, 2 * b) for a, b in every], every, (count, sectors))

    def finish(p, carry):
        value = gelu(sums[p] + b_two[...].reshape(1, 1, feats))
        for r in range(STEP):
            i = STEP * p + r
            out[i] = gather([value[q, STEP * r : STEP * r + STEP] for q in range(sectors)], 0) * mask[i][:, :feats]
        return carry

    second(0, early)
    lax.fori_loop(0, early, finish, 0)
    arrive(north)
    first(bands + 1, 3, 0, sectors + 4)
    no_cells(n_lat - 1, bands + 2)
    second(early, bands - early)
    lax.fori_loop(early, bands, finish, 0)

    last_col.wait_send()
    for dp, copy in [(1, last_row), (1, last_cell)] + east + west_side + south + top + north + corners:
        when(dp, copy.wait_send)


def on_device(n_lat, n_lon, fields, land_sea, w_depth, b_depth, w_one, b_one, w_two, b_two):
    rows, cols = land_sea.shape
    chans, feats = w_one.shape[2:]
    bands, sectors = rows // STEP, cols // STEP
    main = feats // (2 * LANES) * (2 * LANES)
    wide = up_to(feats, LANES)
    halves = chans // LANES
    taps_out_in = jnp.swapaxes(w_one, 2, 3)
    any_space = pl.BlockSpec(memory_space=pltpu.HBM)
    vmem = pl.BlockSpec(memory_space=pltpu.VMEM)
    return pl.pallas_call(
        functools.partial(kernel, (n_lat, n_lon, rows, cols, chans, feats)),
        out_shape=pltpu.VMEM((rows, cols, feats), jnp.float32),
        in_specs=[any_space, vmem, vmem, vmem, any_space, vmem, any_space, vmem],
        out_specs=vmem,
        scratch_shapes=[
            pltpu.VMEM((halves, 2 * rows + 1, 2 * cols + 8, LANES), jnp.float32),
            pltpu.VMEM((halves, 2 * rows, LANES), jnp.float32),
            pltpu.VMEM((halves, 2 * rows, LANES), jnp.float32),
            pltpu.VMEM((halves, 8, LANES), jnp.float32),
            pltpu.VMEM((halves, STEP * rows, LANES), jnp.float32),
            pltpu.VMEM((bands, STEP * STEP, chans), jnp.float32),
            pltpu.VMEM((bands, STEP * STEP, chans), jnp.float32),
            pltpu.VMEM((rows, cols, wide), jnp.float32),
            pltpu.VMEM((bands + 6, sectors + 6, STEP * STEP, chans), jnp.bfloat16),
            pltpu.VMEM((bands + 4, sectors + 4, STEP * STEP, wide), jnp.bfloat16),
            pltpu.VMEM(taps_out_in.shape, jnp.bfloat16),
            pltpu.VMEM((9, chans, feats), jnp.bfloat16),
            pltpu.VMEM(w_two.shape, jnp.bfloat16),
            pltpu.VMEM((9, max(wide - main, LANES), feats), jnp.bfloat16),
            pltpu.VMEM((bands, sectors, STEP * STEP, feats), jnp.float32),
            pltpu.SemaphoreType.DMA((2 + 2 * halves,)),
            pltpu.SemaphoreType.DMA((2, 3)),
            pltpu.SemaphoreType.DMA((2, 12)),
        ],
        compiler_params=pltpu.CompilerParams(
            collective_id=0, has_side_effects=True, vmem_limit_bytes=62 * 1024 * 1024),
    )(fields, land_sea.T, w_depth, b_depth, taps_out_in, b_one, w_two, b_two)


def solution(mesh):
    return jax.shard_map(
        functools.partial(on_device, mesh.shape["lat"], mesh.shape["lon"]),
        mesh=mesh,
        in_specs=(P("lat", "lon", None), P("lat", "lon"), P(), P(), P(), P(), P(), P()),
        out_specs=P("lat", "lon", None),
        check_vma=False,
    )
```

```python
import functools

import jax
import jax.numpy as jnp
from jax import lax
from jax.experimental import pallas as pl
from jax.experimental.pallas import tpu as pltpu
from jax.sharding import PartitionSpec as P

MESH = pl.DeviceIdType.MESH
SIDES = tuple((dp, dq) for dp in (-1, 0, 1) for dq in (-1, 0, 1) if (dp, dq) != (0, 0))
STEP = 4
LANES = 128


def gelu(x):
    return 0.5 * x * (1.0 + lax.erf(x * 0.7071067811865476))


def up_to(value, multiple):
    return -(-value // multiple) * multiple


def kernel(
    shape, fields, land, w_depth, b_depth, w_one, b_one, w_two, b_two, out,
    grid, edge, west, corner, late, open_block, open_sea, mask, down, hidden, one, one_in_out, two, two_tail, sums,
    load_sem, edge_sem, down_sem,
):
    n_lat, n_lon, rows, cols, chans, feats = shape
    bands, sectors = rows // STEP, cols // STEP
    main = feats // (2 * LANES) * (2 * LANES)
    tail = feats - main
    lat, lon = lax.axis_index("lat"), lax.axis_index("lon")
    has = {-1: lat > 0, 0: True, 1: lat < n_lat - 1}

    def when(dp, body):
        if dp == 0:
            body()
        else:
            pl.when(has[dp])(body)

    def device(dp, dq):
        return (lat + dp, lax.rem(lon + dq + n_lon, n_lon))

    halves = chans // LANES
    split = 2 * cols - 8

    def part(h, k):
        start, size = ((split, 8), (0, split))[k]
        return pltpu.make_async_copy(
            fields.at[:, start : start + size, h * LANES : (h + 1) * LANES],
            grid.at[h, 1:, 8 + start : 8 + start + size, :], load_sem.at[2 + 2 * h + k])

    edge_parts = [part(h, 0) for h in range(halves)]
    inner_parts = [part(h, 1) for h in range(halves)]
    load_one = pltpu.make_async_copy(w_one, one, load_sem.at[0])
    load_two = pltpu.make_async_copy(w_two, two, load_sem.at[1])
    for load in edge_parts + inner_parts:
        load.start()

    barrier = pltpu.get_barrier_semaphore()
    for dp, dq in SIDES:
        when(dp, lambda dp=dp, dq=dq: pl.semaphore_signal(
            barrier, inc=1, device_id=device(dp, dq), device_id_type=MESH))

    cells = land[...].astype(jnp.float32)
    for i in range(rows):
        mask[i] = jnp.broadcast_to(cells[:, i : i + 1], mask.shape[1:])

    if tail:
        for p in range(bands + 4):
            hidden[p, :, :, main:] = jnp.zeros(hidden.shape[1:3] + (hidden.shape[3] - main,), hidden.dtype)

    def clear(buffer, width):
        gap = jnp.zeros((width,) + buffer.shape[1:], buffer.dtype)

        def north():
            buffer[0:width] = gap

        def south():
            buffer[buffer.shape[0] - width :] = gap

        pl.when(lat == 0)(north)
        pl.when(lat == n_lat - 1)(south)

    def no_north():
        grid[:, 0, 8:, :] = jnp.zeros((halves, 2 * cols, LANES), grid.dtype)

    pl.when(lat == 0)(no_north)
    clear(down, 3)

    for h in range(halves):
        edge_parts[h].wait()
        for r in range(2 * rows):
            edge[h, r : r + 1, :] = grid[h, 1 + r, 8 + 2 * cols - 1 : 8 + 2 * cols, :]

    pl.semaphore_wait(barrier, 2 + 3 * jnp.minimum(lat, 1) + 3 * jnp.minimum(n_lat - 1 - lat, 1))

    def remote(src, dst, sems, k, dp, dq):
        return pltpu.make_async_remote_copy(
            src_ref=src, dst_ref=dst, send_sem=sems.at[0, k], recv_sem=sems.at[1, k],
            device_id=device(dp, dq), device_id_type=MESH)

    last_row = remote(grid.at[:, 2 * rows, 8:, :], grid.at[:, 0, 8:, :], edge_sem, 0, 1, 0)
    last_col = remote(edge, west, edge_sem, 1, 0, 1)
    last_cell = remote(edge.at[:, 2 * rows - 8 :], corner, edge_sem, 2, 1, 1)
    last_col.start()
    when(1, last_cell.start)
    for inner in inner_parts:
        inner.wait()
    when(1, last_row.start)
    load_one.start()
    load_two.start()

    for h in range(halves):
        grid[h, :, 0:8, :] = jnp.zeros((2 * rows + 1, 8, LANES), grid.dtype)
        late[h] = jnp.zeros(late.shape[1:], late.dtype)

    def down_line(i):
        line = []
        for h in range(halves):
            lanes = slice(h * LANES, (h + 1) * LANES)
            total = jnp.broadcast_to(b_depth[...].reshape(1, chans)[:, lanes], (cols, LANES))
            for a in range(3):
                for b in range(3):
                    piece = grid[h, 2 * i + a, pl.ds(7 + b, cols, stride=2), :]
                    total = total + piece * w_depth[a, b : b + 1, lanes]
            line.append(total)
        return jnp.concatenate(line, axis=1)

    def gather(lines, q):
        return jnp.concatenate([line[STEP * q : STEP * q + STEP] for line in lines], axis=0)

    def down_band(p):
        lines = [down_line(STEP * p + r) for r in range(STEP)]
        seas = [mask[STEP * p + r][:, :chans] for r in range(STEP)]
        masked = [line * sea for line, sea in zip(lines, seas)]
        for q in range(1, sectors):
            down[3 + p, 3 + q] = gather(masked, q).astype(down.dtype)
        return gather(lines, 0), gather(seas, 0)

    def later_band(p, carry):
        block, sea = down_band(p)
        open_block[p] = block
        open_sea[p] = sea
        return carry

    def halo(k, dp, dq, p, count, q, wide):
        src = down.at[3 + p : 3 + p + count, 3 + q : 3 + q + wide]
        to_p, to_q = 3 + p - dp * bands, 3 + q - dq * sectors
        dst = down.at[to_p : to_p + count, to_q : to_q + wide]
        return dp, remote(src, dst, down_sem, k, dp, dq)

    far = bands - 3
    east = [halo(0, 0, 1, far, 3, sectors - 3, 3), halo(1, 0, 1, 1, far - 1, sectors - 3, 3)]
    west_side = [halo(2, 0, -1, far, 3, 0, 3), halo(3, 0, -1, 1, far - 1, 0, 3)]
    south = [halo(4, 1, 0, far, 3, 0, sectors)]
    top = [halo(5, 0, 1, 0, 1, sectors - 3, 3), halo(6, 0, -1, 0, 1, 0, 3)]
    north = [halo(7, -1, 0, 0, 3, 0, sectors)]

    def forward(k, dp, q):
        p, to_p = (3 + far, 0) if dp > 0 else (3, 3 + bands)
        return dp, remote(
            down.at[p : p + 3, q : q + 3], down.at[to_p : to_p + 3, q : q + 3], down_sem, k, dp, 0)

    lower = [forward(8, 1, 0), forward(9, 1, 3 + sectors)]
    upper = [forward(10, -1, 0), forward(11, -1, 3 + sectors)]

    def start(copies):
        for dp, copy in copies:
            when(dp, copy.start)

    def arrive(copies):
        for dp, copy in copies:
            when(-dp, copy.wait_recv)

    lax.fori_loop(1, bands, later_band, 0)
    start(east)

    last_col.wait_recv()
    for h in range(halves):
        lanes = slice(h * LANES, (h + 1) * LANES)
        from_west = sum(
            west[h, pl.ds(8 * STEP // 4 - 1 + a, rows - STEP, stride=2), :] * w_depth[a, 0:1, lanes]
            for a in range(3))
        late[h, pl.ds(STEP * STEP, rows - STEP, stride=STEP), :] = from_west
    for p in range(1, bands):
        extra = jnp.concatenate(
            [late[h, STEP * STEP * p : STEP * STEP * (p + 1), :] for h in range(halves)], axis=1)
        down[3 + p, 3] = ((open_block[p] + extra) * open_sea[p]).astype(down.dtype)

    start(west_side + south)

    def from_north():
        last_row.wait_recv()
        last_cell.wait_recv()
        for h in range(halves):
            grid[h, 0, 7:8, :] = corner[h, 7:8, :]

    for h in range(halves):
        for r in range(2 * STEP):
            grid[h, 1 + r, 7:8, :] = west[h, r : r + 1, :]
    pl.when(has[-1])(from_north)
    block, sea = down_band(0)
    down[3, 3] = (block * sea).astype(down.dtype)

    start(top + north)

    def first(p, count, q, wide):
        flat = count * wide * STEP * STEP
        pieces = [
            down[p + a : p + a + count, q + b : q + b + wide].reshape(flat, chans)
            for a in range(3) for b in range(3)
        ]
        total = jnp.dot(
            jnp.concatenate(pieces, axis=1), one_in_out[...].reshape(9 * chans, feats),
            preferred_element_type=jnp.float32)
        value = gelu(total + b_one[...].reshape(1, feats)).astype(hidden.dtype)
        hidden[p : p + count, q : q + wide, :, 0:feats] = value.reshape(
            count, wide, STEP * STEP, feats)

    load_one.wait()

    def turn(t, carry):
        tap = one.at[t // 3, lax.rem(t, 3)]
        one_in_out[t, :, 0:main] = jnp.transpose(tap[0:main, :])
        if tail:
            rest = jnp.concatenate(
                [tap[main:feats, :], jnp.zeros((up_to(tail, LANES) - tail, chans), one.dtype)], axis=0)
            one_in_out[t, :, main:feats] = jnp.transpose(rest)[:, 0:tail]
        return carry

    lax.fori_loop(0, 9, turn, 0)
    first(3, bands - 2, 3, sectors - 2)
    arrive(east[:1] + west_side[:1])
    start(lower)
    load_two.wait()
    if tail:
        for t in range(9):
            two_tail[t] = jnp.zeros(two_tail.shape[1:], two_tail.dtype)
            two_tail[t, 0:tail, :] = two[t // 3, t % 3, main:feats, :]
    arrive(east[1:] + top[:1])
    start(upper[:1])
    first(3, bands - 2, 0, 3)
    arrive(west_side[1:] + top[1:])
    start(upper[1:])
    first(3, bands - 2, sectors + 1, 3)
    arrive(south + lower)
    first(0, 3, 0, sectors + 4)

    def no_cells(lat_at, p):
        def body():
            hidden[p : p + 2] = jnp.zeros((2,) + hidden.shape[1:], hidden.dtype)

        pl.when(lat == lat_at)(body)

    no_cells(0, 0)

    def taps_of(buffer, places, taps, size):
        count = size[0] * size[1] * STEP * STEP
        window = [
            buffer[pl.ds(p, size[0]), q : q + size[1]].reshape(count, buffer.shape[3])
            for p, q in places
        ]
        total = jnp.dot(
            jnp.concatenate([cells[:, 0:main] for cells in window], axis=1),
            jnp.concatenate([two[a, b, 0:main, :] for a, b in taps], axis=0),
            preferred_element_type=jnp.float32)
        if tail:
            total = total + jnp.dot(
                jnp.concatenate([cells[:, main:] for cells in window], axis=1),
                jnp.concatenate([two_tail[3 * a + b] for a, b in taps], axis=0),
                preferred_element_type=jnp.float32)
        return total.reshape(size + (STEP * STEP, feats))

    every = [(a, b) for a in range(3) for b in range(3)]
    early = bands - 3

    def second(p, count):
        sums[p : p + count] = taps_of(
            hidden, [(p + 2 * a, 2 * b) for a, b in every], every, (count, sectors))

    def finish(p, carry):
        value = gelu(sums[p] + b_two[...].reshape(1, 1, feats))
        for r in range(STEP):
            i = STEP * p + r
            out[i] = gather([value[q, STEP * r : STEP * r + STEP] for q in range(sectors)], 0) * mask[i][:, :feats]
        return carry

    second(0, early)
    lax.fori_loop(0, early, finish, 0)
    arrive(north + upper)
    first(bands + 1, 3, 0, sectors + 4)
    no_cells(n_lat - 1, bands + 2)
    second(early, bands - early)
    lax.fori_loop(early, bands, finish, 0)

    last_col.wait_send()
    for dp, copy in [(1, last_row), (1, last_cell)] + east + west_side + south + top + north + lower + upper:
        when(dp, copy.wait_send)


def on_device(n_lat, n_lon, fields, land_sea, w_depth, b_depth, w_one, b_one, w_two, b_two):
    rows, cols = land_sea.shape
    chans, feats = w_one.shape[2:]
    bands, sectors = rows // STEP, cols // STEP
    main = feats // (2 * LANES) * (2 * LANES)
    wide = up_to(feats, LANES)
    halves = chans // LANES
    taps_out_in = jnp.swapaxes(w_one, 2, 3)
    any_space = pl.BlockSpec(memory_space=pltpu.HBM)
    vmem = pl.BlockSpec(memory_space=pltpu.VMEM)
    return pl.pallas_call(
        functools.partial(kernel, (n_lat, n_lon, rows, cols, chans, feats)),
        out_shape=pltpu.VMEM((rows, cols, feats), jnp.float32),
        in_specs=[any_space, vmem, vmem, vmem, any_space, vmem, any_space, vmem],
        out_specs=vmem,
        scratch_shapes=[
            pltpu.VMEM((halves, 2 * rows + 1, 2 * cols + 8, LANES), jnp.float32),
            pltpu.VMEM((halves, 2 * rows, LANES), jnp.float32),
            pltpu.VMEM((halves, 2 * rows, LANES), jnp.float32),
            pltpu.VMEM((halves, 8, LANES), jnp.float32),
            pltpu.VMEM((halves, STEP * rows, LANES), jnp.float32),
            pltpu.VMEM((bands, STEP * STEP, chans), jnp.float32),
            pltpu.VMEM((bands, STEP * STEP, chans), jnp.float32),
            pltpu.VMEM((rows, cols, wide), jnp.float32),
            pltpu.VMEM((bands + 6, sectors + 6, STEP * STEP, chans), jnp.bfloat16),
            pltpu.VMEM((bands + 4, sectors + 4, STEP * STEP, wide), jnp.bfloat16),
            pltpu.VMEM(taps_out_in.shape, jnp.bfloat16),
            pltpu.VMEM((9, chans, feats), jnp.bfloat16),
            pltpu.VMEM(w_two.shape, jnp.bfloat16),
            pltpu.VMEM((9, max(wide - main, LANES), feats), jnp.bfloat16),
            pltpu.VMEM((bands, sectors, STEP * STEP, feats), jnp.float32),
            pltpu.SemaphoreType.DMA((2 + 2 * halves,)),
            pltpu.SemaphoreType.DMA((2, 3)),
            pltpu.SemaphoreType.DMA((2, 12)),
        ],
        compiler_params=pltpu.CompilerParams(
            collective_id=0, has_side_effects=True, vmem_limit_bytes=62 * 1024 * 1024),
    )(fields, land_sea.T, w_depth, b_depth, taps_out_in, b_one, w_two, b_two)


def solution(mesh):
    return jax.shard_map(
        functools.partial(on_device, mesh.shape["lat"], mesh.shape["lon"]),
        mesh=mesh,
        in_specs=(P("lat", "lon", None), P("lat", "lon"), P(), P(), P(), P(), P(), P()),
        out_specs=P("lat", "lon", None),
        check_vma=False,
    )
```

```python
import functools

import jax
import jax.numpy as jnp
from jax import lax
from jax.experimental import pallas as pl
from jax.experimental.pallas import tpu as pltpu
from jax.sharding import PartitionSpec as P

MESH = pl.DeviceIdType.MESH
SIDES = tuple((dp, dq) for dp in (-1, 0, 1) for dq in (-1, 0, 1) if (dp, dq) != (0, 0))
STEP = 4
LANES = 128


def gelu(x):
    return 0.5 * x * (1.0 + lax.erf(x * 0.7071067811865476))


def up_to(value, multiple):
    return -(-value // multiple) * multiple


def kernel(
    shape, fields, land, w_depth, b_depth, w_one, b_one, w_two, b_two, out,
    grid, edge, west, edge_sent, west_sent, corner, late, open_block, open_sea, mask, down, hidden, one, one_in_out, two, two_tail, sums,
    load_sem, edge_sem, down_sem,
):
    n_lat, n_lon, rows, cols, chans, feats = shape
    bands, sectors = rows // STEP, cols // STEP
    main = feats // (2 * LANES) * (2 * LANES)
    tail = feats - main
    lat, lon = lax.axis_index("lat"), lax.axis_index("lon")
    has = {-1: lat > 0, 0: True, 1: lat < n_lat - 1}

    def when(dp, body):
        if dp == 0:
            body()
        else:
            pl.when(has[dp])(body)

    def device(dp, dq):
        return (lat + dp, lax.rem(lon + dq + n_lon, n_lon))

    halves = chans // LANES
    split = 2 * cols - 8

    def part(h, k):
        start, size = ((split, 8), (0, split))[k]
        return pltpu.make_async_copy(
            fields.at[:, start : start + size, h * LANES : (h + 1) * LANES],
            grid.at[h, 1:, 8 + start : 8 + start + size, :], load_sem.at[2 + 2 * h + k])

    edge_parts = [part(h, 0) for h in range(halves)]
    inner_parts = [part(h, 1) for h in range(halves)]
    load_one = pltpu.make_async_copy(w_one, one, load_sem.at[0])
    load_two = pltpu.make_async_copy(w_two, two, load_sem.at[1])
    for load in edge_parts + inner_parts:
        load.start()

    barrier = pltpu.get_barrier_semaphore()
    for dp, dq in SIDES:
        when(dp, lambda dp=dp, dq=dq: pl.semaphore_signal(
            barrier, inc=1, device_id=device(dp, dq), device_id_type=MESH))

    cells = land[...].astype(jnp.float32)
    for i in range(rows):
        mask[i] = jnp.broadcast_to(cells[:, i : i + 1], mask.shape[1:])

    if tail:
        for p in range(bands + 4):
            hidden[p, :, :, main:] = jnp.zeros(hidden.shape[1:3] + (hidden.shape[3] - main,), hidden.dtype)

    def clear(buffer, width):
        gap = jnp.zeros((width,) + buffer.shape[1:], buffer.dtype)

        def north():
            buffer[0:width] = gap

        def south():
            buffer[buffer.shape[0] - width :] = gap

        pl.when(lat == 0)(north)
        pl.when(lat == n_lat - 1)(south)

    def no_north():
        grid[:, 0, 8:, :] = jnp.zeros((halves, 2 * cols, LANES), grid.dtype)

    pl.when(lat == 0)(no_north)
    clear(down, 3)

    for h in range(halves):
        edge_parts[h].wait()
        for r in range(2 * rows):
            edge[h, r : r + 1, :] = grid[h, 1 + r, 8 + 2 * cols - 1 : 8 + 2 * cols, :]
    edge_sent[...] = edge[...].astype(edge_sent.dtype)

    pl.semaphore_wait(barrier, 2 + 3 * jnp.minimum(lat, 1) + 3 * jnp.minimum(n_lat - 1 - lat, 1))

    def remote(src, dst, sems, k, dp, dq):
        return pltpu.make_async_remote_copy(
            src_ref=src, dst_ref=dst, send_sem=sems.at[0, k], recv_sem=sems.at[1, k],
            device_id=device(dp, dq), device_id_type=MESH)

    last_row = remote(grid.at[:, 2 * rows, 8:, :], grid.at[:, 0, 8:, :], edge_sem, 0, 1, 0)
    last_col = remote(edge_sent, west_sent, edge_sem, 1, 0, 1)
    last_cell = remote(edge_sent.at[:, 2 * rows - 16 :], corner, edge_sem, 2, 1, 1)
    last_col.start()
    when(1, last_cell.start)
    for inner in inner_parts:
        inner.wait()
    when(1, last_row.start)
    load_one.start()
    load_two.start()

    for h in range(halves):
        grid[h, :, 0:8, :] = jnp.zeros((2 * rows + 1, 8, LANES), grid.dtype)
        late[h] = jnp.zeros(late.shape[1:], late.dtype)

    def down_line(i):
        line = []
        for h in range(halves):
            lanes = slice(h * LANES, (h + 1) * LANES)
            total = jnp.broadcast_to(b_depth[...].reshape(1, chans)[:, lanes], (cols, LANES))
            for a in range(3):
                for b in range(3):
                    piece = grid[h, 2 * i + a, pl.ds(7 + b, cols, stride=2), :]
                    total = total + piece * w_depth[a, b : b + 1, lanes]
            line.append(total)
        return jnp.concatenate(line, axis=1)

    def gather(lines, q):
        return jnp.concatenate([line[STEP * q : STEP * q + STEP] for line in lines], axis=0)

    def down_band(p):
        lines = [down_line(STEP * p + r) for r in range(STEP)]
        seas = [mask[STEP * p + r][:, :chans] for r in range(STEP)]
        masked = [line * sea for line, sea in zip(lines, seas)]
        for q in range(1, sectors):
            down[3 + p, 3 + q] = gather(masked, q).astype(down.dtype)
        return gather(lines, 0), gather(seas, 0)

    def later_band(p, carry):
        block, sea = down_band(p)
        open_block[p] = block
        open_sea[p] = sea
        return carry

    def halo(k, dp, dq, p, count, q, wide):
        src = down.at[3 + p : 3 + p + count, 3 + q : 3 + q + wide]
        to_p, to_q = 3 + p - dp * bands, 3 + q - dq * sectors
        dst = down.at[to_p : to_p + count, to_q : to_q + wide]
        return dp, remote(src, dst, down_sem, k, dp, dq)

    far = bands - 3
    east = [halo(0, 0, 1, far, 3, sectors - 3, 3), halo(1, 0, 1, 1, far - 1, sectors - 3, 3)]
    west_side = [halo(2, 0, -1, far, 3, 0, 3), halo(3, 0, -1, 1, far - 1, 0, 3)]
    south = [halo(4, 1, 0, far, 3, 0, sectors)]
    top = [halo(5, 0, 1, 0, 1, sectors - 3, 3), halo(6, 0, -1, 0, 1, 0, 3)]
    north = [halo(7, -1, 0, 0, 3, 0, sectors), halo(8, -1, 1, 0, 3, sectors - 3, 3),
             halo(9, -1, -1, 0, 3, 0, 3)]

    def forward(k, q):
        return 1, remote(down.at[3 + far : 6 + far, q : q + 3], down.at[0:3, q : q + 3], down_sem, k, 1, 0)

    corners = [forward(10, 0), forward(11, 3 + sectors)]

    def start(copies):
        for dp, copy in copies:
            when(dp, copy.start)

    def arrive(copies):
        for dp, copy in copies:
            when(-dp, copy.wait_recv)

    lax.fori_loop(1, bands, later_band, 0)
    start(east)

    last_col.wait_recv()
    west[...] = west_sent[...].astype(west.dtype)
    for h in range(halves):
        lanes = slice(h * LANES, (h + 1) * LANES)
        from_west = sum(
            west[h, pl.ds(8 * STEP // 4 - 1 + a, rows - STEP, stride=2), :] * w_depth[a, 0:1, lanes]
            for a in range(3))
        late[h, pl.ds(STEP * STEP, rows - STEP, stride=STEP), :] = from_west
    for p in range(1, bands):
        extra = jnp.concatenate(
            [late[h, STEP * STEP * p : STEP * STEP * (p + 1), :] for h in range(halves)], axis=1)
        down[3 + p, 3] = ((open_block[p] + extra) * open_sea[p]).astype(down.dtype)

    start(west_side + south)

    def from_north():
        last_row.wait_recv()
        last_cell.wait_recv()
        for h in range(halves):
            grid[h, 0, 7:8, :] = corner[h].astype(grid.dtype)[15:16, :]

    for h in range(halves):
        for r in range(2 * STEP):
            grid[h, 1 + r, 7:8, :] = west[h, r : r + 1, :]
    pl.when(has[-1])(from_north)
    block, sea = down_band(0)
    down[3, 3] = (block * sea).astype(down.dtype)

    start(top + north)

    def first(p, count, q, wide):
        flat = count * wide * STEP * STEP
        pieces = [
            down[p + a : p + a + count, q + b : q + b + wide].reshape(flat, chans)
            for a in range(3) for b in range(3)
        ]
        total = jnp.dot(
            jnp.concatenate(pieces, axis=1), one_in_out[...].reshape(9 * chans, feats),
            preferred_element_type=jnp.float32)
        value = gelu(total + b_one[...].reshape(1, feats)).astype(hidden.dtype)
        hidden[p : p + count, q : q + wide, :, 0:feats] = value.reshape(
            count, wide, STEP * STEP, feats)

    load_one.wait()

    def turn(t, carry):
        tap = one.at[t // 3, lax.rem(t, 3)]
        one_in_out[t, :, 0:main] = jnp.transpose(tap[0:main, :])
        if tail:
            rest = jnp.concatenate(
                [tap[main:feats, :], jnp.zeros((up_to(tail, LANES) - tail, chans), one.dtype)], axis=0)
            one_in_out[t, :, main:feats] = jnp.transpose(rest)[:, 0:tail]
        return carry

    lax.fori_loop(0, 9, turn, 0)
    first(3, bands - 2, 3, sectors - 2)
    arrive(east[:1] + west_side[:1])
    start(corners)
    load_two.wait()
    if tail:
        for t in range(9):
            two_tail[t] = jnp.zeros(two_tail.shape[1:], two_tail.dtype)
            two_tail[t, 0:tail, :] = two[t // 3, t % 3, main:feats, :]
    arrive(east[1:] + top[:1])
    first(3, bands - 2, 0, 3)
    arrive(west_side[1:] + top[1:])
    first(3, bands - 2, sectors + 1, 3)
    arrive(south + corners)
    first(0, 3, 0, sectors + 4)

    def no_cells(lat_at, p):
        def body():
            hidden[p : p + 2] = jnp.zeros((2,) + hidden.shape[1:], hidden.dtype)

        pl.when(lat == lat_at)(body)

    no_cells(0, 0)

    def taps_of(buffer, places, taps, size):
        count = size[0] * size[1] * STEP * STEP
        window = [
            buffer[pl.ds(p, size[0]), q : q + size[1]].reshape(count, buffer.shape[3])
            for p, q in places
        ]
        total = jnp.dot(
            jnp.concatenate([cells[:, 0:main] for cells in window], axis=1),
            jnp.concatenate([two[a, b, 0:main, :] for a, b in taps], axis=0),
            preferred_element_type=jnp.float32)
        if tail:
            total = total + jnp.dot(
                jnp.concatenate([cells[:, main:] for cells in window], axis=1),
                jnp.concatenate([two_tail[3 * a + b] for a, b in taps], axis=0),
                preferred_element_type=jnp.float32)
        return total.reshape(size + (STEP * STEP, feats))

    every = [(a, b) for a in range(3) for b in range(3)]
    early = bands - 3

    def second(p, count):
        sums[p : p + count] = taps_of(
            hidden, [(p + 2 * a, 2 * b) for a, b in every], every, (count, sectors))

    def finish(p, carry):
        value = gelu(sums[p] + b_two[...].reshape(1, 1, feats))
        for r in range(STEP):
            i = STEP * p + r
            out[i] = gather([value[q, STEP * r : STEP * r + STEP] for q in range(sectors)], 0) * mask[i][:, :feats]
        return carry

    second(0, early)
    lax.fori_loop(0, early, finish, 0)
    arrive(north)
    first(bands + 1, 3, 0, sectors + 4)
    no_cells(n_lat - 1, bands + 2)
    second(early, bands - early)
    lax.fori_loop(early, bands, finish, 0)

    last_col.wait_send()
    for dp, copy in [(1, last_row), (1, last_cell)] + east + west_side + south + top + north + corners:
        when(dp, copy.wait_send)


def on_device(n_lat, n_lon, fields, land_sea, w_depth, b_depth, w_one, b_one, w_two, b_two):
    rows, cols = land_sea.shape
    chans, feats = w_one.shape[2:]
    bands, sectors = rows // STEP, cols // STEP
    main = feats // (2 * LANES) * (2 * LANES)
    wide = up_to(feats, LANES)
    halves = chans // LANES
    taps_out_in = jnp.swapaxes(w_one, 2, 3)
    any_space = pl.BlockSpec(memory_space=pltpu.HBM)
    vmem = pl.BlockSpec(memory_space=pltpu.VMEM)
    return pl.pallas_call(
        functools.partial(kernel, (n_lat, n_lon, rows, cols, chans, feats)),
        out_shape=pltpu.VMEM((rows, cols, feats), jnp.float32),
        in_specs=[any_space, vmem, vmem, vmem, any_space, vmem, any_space, vmem],
        out_specs=vmem,
        scratch_shapes=[
            pltpu.VMEM((halves, 2 * rows + 1, 2 * cols + 8, LANES), jnp.float32),
            pltpu.VMEM((halves, 2 * rows, LANES), jnp.float32),
            pltpu.VMEM((halves, 2 * rows, LANES), jnp.float32),
            pltpu.VMEM((halves, 2 * rows, LANES), jnp.bfloat16),
            pltpu.VMEM((halves, 2 * rows, LANES), jnp.bfloat16),
            pltpu.VMEM((halves, 16, LANES), jnp.bfloat16),
            pltpu.VMEM((halves, STEP * rows, LANES), jnp.float32),
            pltpu.VMEM((bands, STEP * STEP, chans), jnp.float32),
            pltpu.VMEM((bands, STEP * STEP, chans), jnp.float32),
            pltpu.VMEM((rows, cols, wide), jnp.float32),
            pltpu.VMEM((bands + 6, sectors + 6, STEP * STEP, chans), jnp.bfloat16),
            pltpu.VMEM((bands + 4, sectors + 4, STEP * STEP, wide), jnp.bfloat16),
            pltpu.VMEM(taps_out_in.shape, jnp.bfloat16),
            pltpu.VMEM((9, chans, feats), jnp.bfloat16),
            pltpu.VMEM(w_two.shape, jnp.bfloat16),
            pltpu.VMEM((9, max(wide - main, LANES), feats), jnp.bfloat16),
            pltpu.VMEM((bands, sectors, STEP * STEP, feats), jnp.float32),
            pltpu.SemaphoreType.DMA((2 + 2 * halves,)),
            pltpu.SemaphoreType.DMA((2, 3)),
            pltpu.SemaphoreType.DMA((2, 12)),
        ],
        compiler_params=pltpu.CompilerParams(
            collective_id=0, has_side_effects=True, vmem_limit_bytes=62 * 1024 * 1024),
    )(fields, land_sea.T, w_depth, b_depth, taps_out_in, b_one, w_two, b_two)


def solution(mesh):
    return jax.shard_map(
        functools.partial(on_device, mesh.shape["lat"], mesh.shape["lon"]),
        mesh=mesh,
        in_specs=(P("lat", "lon", None), P("lat", "lon"), P(), P(), P(), P(), P(), P()),
        out_specs=P("lat", "lon", None),
        check_vma=False,
    )
```

```python
import functools

import jax
import jax.numpy as jnp
from jax import lax
from jax.experimental import pallas as pl
from jax.experimental.pallas import tpu as pltpu
from jax.sharding import PartitionSpec as P

MESH = pl.DeviceIdType.MESH
SIDES = tuple((dp, dq) for dp in (-1, 0, 1) for dq in (-1, 0, 1) if (dp, dq) != (0, 0))
STEP = 4
LANES = 128


def gelu(x):
    return 0.5 * x * (1.0 + lax.erf(x * 0.7071067811865476))


def up_to(value, multiple):
    return -(-value // multiple) * multiple


def kernel(
    shape, fields, land, w_depth, b_depth, w_one, b_one, w_two, b_two, out,
    grid, edge, west, edge_sent, west_sent, corner, late, open_block, open_sea, mask, down, hidden, one, one_in_out, two, two_tail, sums,
    load_sem, edge_sem, down_sem,
):
    n_lat, n_lon, rows, cols, chans, feats = shape
    bands, sectors = rows // STEP, cols // STEP
    main = feats // (2 * LANES) * (2 * LANES)
    tail = feats - main
    lat, lon = lax.axis_index("lat"), lax.axis_index("lon")
    has = {-1: lat > 0, 0: True, 1: lat < n_lat - 1}

    def when(dp, body):
        if dp == 0:
            body()
        else:
            pl.when(has[dp])(body)

    def device(dp, dq):
        return (lat + dp, lax.rem(lon + dq + n_lon, n_lon))

    halves = chans // LANES
    split = 2 * cols - 8

    def part(h, k):
        start, size = ((split, 8), (0, split))[k]
        return pltpu.make_async_copy(
            fields.at[:, start : start + size, h * LANES : (h + 1) * LANES],
            grid.at[h, 1:, 8 + start : 8 + start + size, :], load_sem.at[2 + 2 * h + k])

    edge_parts = [part(h, 0) for h in range(halves)]
    inner_parts = [part(h, 1) for h in range(halves)]
    load_one = pltpu.make_async_copy(w_one, one, load_sem.at[0])
    load_two = pltpu.make_async_copy(w_two, two, load_sem.at[1])
    for load in edge_parts + inner_parts:
        load.start()

    barrier = pltpu.get_barrier_semaphore()
    for dp, dq in SIDES:
        when(dp, lambda dp=dp, dq=dq: pl.semaphore_signal(
            barrier, inc=1, device_id=device(dp, dq), device_id_type=MESH))

    cells = land[...].astype(jnp.float32)
    for i in range(rows):
        mask[i] = jnp.broadcast_to(cells[:, i : i + 1], mask.shape[1:])

    if tail:
        for p in range(bands + 4):
            hidden[p, :, :, main:] = jnp.zeros(hidden.shape[1:3] + (hidden.shape[3] - main,), hidden.dtype)

    def clear(buffer, width):
        gap = jnp.zeros((width,) + buffer.shape[1:], buffer.dtype)

        def north():
            buffer[0:width] = gap

        def south():
            buffer[buffer.shape[0] - width :] = gap

        pl.when(lat == 0)(north)
        pl.when(lat == n_lat - 1)(south)

    def no_north():
        grid[:, 0, 8:, :] = jnp.zeros((halves, 2 * cols, LANES), grid.dtype)

    pl.when(lat == 0)(no_north)
    clear(down, 3)

    for h in range(halves):
        edge_parts[h].wait()
        for r in range(2 * rows):
            edge[h, r : r + 1, :] = grid[h, 1 + r, 8 + 2 * cols - 1 : 8 + 2 * cols, :]
    edge_sent[...] = edge[...].astype(edge_sent.dtype)

    pl.semaphore_wait(barrier, 2 + 3 * jnp.minimum(lat, 1) + 3 * jnp.minimum(n_lat - 1 - lat, 1))

    def remote(src, dst, sems, k, dp, dq):
        return pltpu.make_async_remote_copy(
            src_ref=src, dst_ref=dst, send_sem=sems.at[0, k], recv_sem=sems.at[1, k],
            device_id=device(dp, dq), device_id_type=MESH)

    last_row = remote(grid.at[:, 2 * rows, 8:, :], grid.at[:, 0, 8:, :], edge_sem, 0, 1, 0)
    last_col = remote(edge_sent, west_sent, edge_sem, 1, 0, 1)
    last_cell = remote(edge_sent.at[:, 2 * rows - 16 :], corner, edge_sem, 2, 1, 1)
    last_col.start()
    when(1, last_cell.start)
    for inner in inner_parts:
        inner.wait()
    when(1, last_row.start)
    load_one.start()
    load_two.start()

    for h in range(halves):
        grid[h, :, 0:8, :] = jnp.zeros((2 * rows + 1, 8, LANES), grid.dtype)
        late[h] = jnp.zeros(late.shape[1:], late.dtype)

    def down_line(i):
        line = []
        for h in range(halves):
            lanes = slice(h * LANES, (h + 1) * LANES)
            total = jnp.broadcast_to(b_depth[...].reshape(1, chans)[:, lanes], (cols, LANES))
            for a in range(3):
                for b in range(3):
                    piece = grid[h, 2 * i + a, pl.ds(7 + b, cols, stride=2), :]
                    total = total + piece * w_depth[a, b : b + 1, lanes]
            line.append(total)
        return jnp.concatenate(line, axis=1)

    def gather(lines, q):
        return jnp.concatenate([line[STEP * q : STEP * q + STEP] for line in lines], axis=0)

    def down_band(p):
        lines = [down_line(STEP * p + r) for r in range(STEP)]
        seas = [mask[STEP * p + r][:, :chans] for r in range(STEP)]
        masked = [line * sea for line, sea in zip(lines, seas)]
        for q in range(1, sectors):
            down[3 + p, 3 + q] = gather(masked, q).astype(down.dtype)
        return gather(lines, 0), gather(seas, 0)

    def later_band(p, carry):
        block, sea = down_band(p)
        open_block[p] = block
        open_sea[p] = sea
        return carry

    def halo(k, dp, dq, p, count, q, wide):
        src = down.at[3 + p : 3 + p + count, 3 + q : 3 + q + wide]
        to_p, to_q = 3 + p - dp * bands, 3 + q - dq * sectors
        dst = down.at[to_p : to_p + count, to_q : to_q + wide]
        return dp, remote(src, dst, down_sem, k, dp, dq)

    far = bands - 3
    east = [halo(0, 0, 1, far, 3, sectors - 3, 3), halo(1, 0, 1, 1, far - 1, sectors - 3, 3)]
    west_side = [halo(2, 0, -1, far, 3, 0, 3), halo(3, 0, -1, 1, far - 1, 0, 3)]
    south = [halo(4, 1, 0, far, 3, 0, sectors)]
    top = [halo(5, 0, 1, 0, 1, sectors - 3, 3), halo(6, 0, -1, 0, 1, 0, 3)]
    north = [halo(7, -1, 0, 0, 3, 0, sectors), halo(8, -1, 1, 0, 3, sectors - 3, 3),
             halo(9, -1, -1, 0, 3, 0, 3)]

    def forward(k, q):
        return 1, remote(down.at[3 + far : 6 + far, q : q + 3], down.at[0:3, q : q + 3], down_sem, k, 1, 0)

    corners = [forward(10, 0), forward(11, 3 + sectors)]

    def start(copies):
        for dp, copy in copies:
            when(dp, copy.start)

    def arrive(copies):
        for dp, copy in copies:
            when(-dp, copy.wait_recv)

    lax.fori_loop(1, bands, later_band, 0)
    start(east)

    last_col.wait_recv()
    west[...] = west_sent[...].astype(west.dtype)
    for h in range(halves):
        lanes = slice(h * LANES, (h + 1) * LANES)
        from_west = sum(
            west[h, pl.ds(8 * STEP // 4 - 1 + a, rows - STEP, stride=2), :] * w_depth[a, 0:1, lanes]
            for a in range(3))
        late[h, pl.ds(STEP * STEP, rows - STEP, stride=STEP), :] = from_west
    for p in range(1, bands):
        extra = jnp.concatenate(
            [late[h, STEP * STEP * p : STEP * STEP * (p + 1), :] for h in range(halves)], axis=1)
        down[3 + p, 3] = ((open_block[p] + extra) * open_sea[p]).astype(down.dtype)

    start(west_side + south)

    def from_north():
        last_row.wait_recv()
        last_cell.wait_recv()
        for h in range(halves):
            grid[h, 0, 7:8, :] = corner[h].astype(grid.dtype)[15:16, :]

    for h in range(halves):
        for r in range(2 * STEP):
            grid[h, 1 + r, 7:8, :] = west[h, r : r + 1, :]
    pl.when(has[-1])(from_north)
    block, sea = down_band(0)
    down[3, 3] = (block * sea).astype(down.dtype)

    start(top[1:] + north[2:] + top[:1] + north[1:2] + north[:1])

    def first(p, count, q, wide):
        flat = count * wide * STEP * STEP
        pieces = [
            down[p + a : p + a + count, q + b : q + b + wide].reshape(flat, chans)
            for a in range(3) for b in range(3)
        ]
        total = jnp.dot(
            jnp.concatenate(pieces, axis=1), one_in_out[...].reshape(9 * chans, feats),
            preferred_element_type=jnp.float32)
        value = gelu(total + b_one[...].reshape(1, feats)).astype(hidden.dtype)
        hidden[p : p + count, q : q + wide, :, 0:feats] = value.reshape(
            count, wide, STEP * STEP, feats)

    load_one.wait()

    def turn(t, carry):
        tap = one.at[t // 3, lax.rem(t, 3)]
        one_in_out[t, :, 0:main] = jnp.transpose(tap[0:main, :])
        if tail:
            rest = jnp.concatenate(
                [tap[main:feats, :], jnp.zeros((up_to(tail, LANES) - tail, chans), one.dtype)], axis=0)
            one_in_out[t, :, main:feats] = jnp.transpose(rest)[:, 0:tail]
        return carry

    lax.fori_loop(0, 9, turn, 0)
    first(3, bands - 2, 3, sectors - 2)
    arrive(east[:1] + west_side[:1])
    start(corners)
    load_two.wait()
    if tail:
        for t in range(9):
            two_tail[t] = jnp.zeros(two_tail.shape[1:], two_tail.dtype)
            two_tail[t, 0:tail, :] = two[t // 3, t % 3, main:feats, :]
    arrive(east[1:] + top[:1])
    first(3, bands - 2, 0, 3)
    arrive(west_side[1:] + top[1:])
    first(3, bands - 2, sectors + 1, 3)
    arrive(south + corners)
    first(0, 3, 0, sectors + 4)

    def no_cells(lat_at, p):
        def body():
            hidden[p : p + 2] = jnp.zeros((2,) + hidden.shape[1:], hidden.dtype)

        pl.when(lat == lat_at)(body)

    no_cells(0, 0)

    def taps_of(buffer, places, taps, size):
        count = size[0] * size[1] * STEP * STEP
        window = [
            buffer[pl.ds(p, size[0]), q : q + size[1]].reshape(count, buffer.shape[3])
            for p, q in places
        ]
        total = jnp.dot(
            jnp.concatenate([cells[:, 0:main] for cells in window], axis=1),
            jnp.concatenate([two[a, b, 0:main, :] for a, b in taps], axis=0),
            preferred_element_type=jnp.float32)
        if tail:
            total = total + jnp.dot(
                jnp.concatenate([cells[:, main:] for cells in window], axis=1),
                jnp.concatenate([two_tail[3 * a + b] for a, b in taps], axis=0),
                preferred_element_type=jnp.float32)
        return total.reshape(size + (STEP * STEP, feats))

    every = [(a, b) for a in range(3) for b in range(3)]
    early = bands - 3

    def second(p, count):
        sums[p : p + count] = taps_of(
            hidden, [(p + 2 * a, 2 * b) for a, b in every], every, (count, sectors))

    def finish(p, carry):
        value = gelu(sums[p] + b_two[...].reshape(1, 1, feats))
        for r in range(STEP):
            i = STEP * p + r
            out[i] = gather([value[q, STEP * r : STEP * r + STEP] for q in range(sectors)], 0) * mask[i][:, :feats]
        return carry

    second(0, early)
    lax.fori_loop(0, early, finish, 0)
    arrive(north)
    first(bands + 1, 3, 0, sectors + 4)
    no_cells(n_lat - 1, bands + 2)
    second(early, bands - early)
    lax.fori_loop(early, bands, finish, 0)

    last_col.wait_send()
    for dp, copy in [(1, last_row), (1, last_cell)] + east + west_side + south + top + north + corners:
        when(dp, copy.wait_send)


def on_device(n_lat, n_lon, fields, land_sea, w_depth, b_depth, w_one, b_one, w_two, b_two):
    rows, cols = land_sea.shape
    chans, feats = w_one.shape[2:]
    bands, sectors = rows // STEP, cols // STEP
    main = feats // (2 * LANES) * (2 * LANES)
    wide = up_to(feats, LANES)
    halves = chans // LANES
    taps_out_in = jnp.swapaxes(w_one, 2, 3)
    any_space = pl.BlockSpec(memory_space=pltpu.HBM)
    vmem = pl.BlockSpec(memory_space=pltpu.VMEM)
    return pl.pallas_call(
        functools.partial(kernel, (n_lat, n_lon, rows, cols, chans, feats)),
        out_shape=pltpu.VMEM((rows, cols, feats), jnp.float32),
        in_specs=[any_space, vmem, vmem, vmem, any_space, vmem, any_space, vmem],
        out_specs=vmem,
        scratch_shapes=[
            pltpu.VMEM((halves, 2 * rows + 1, 2 * cols + 8, LANES), jnp.float32),
            pltpu.VMEM((halves, 2 * rows, LANES), jnp.float32),
            pltpu.VMEM((halves, 2 * rows, LANES), jnp.float32),
            pltpu.VMEM((halves, 2 * rows, LANES), jnp.bfloat16),
            pltpu.VMEM((halves, 2 * rows, LANES), jnp.bfloat16),
            pltpu.VMEM((halves, 16, LANES), jnp.bfloat16),
            pltpu.VMEM((halves, STEP * rows, LANES), jnp.float32),
            pltpu.VMEM((bands, STEP * STEP, chans), jnp.float32),
            pltpu.VMEM((bands, STEP * STEP, chans), jnp.float32),
            pltpu.VMEM((rows, cols, wide), jnp.float32),
            pltpu.VMEM((bands + 6, sectors + 6, STEP * STEP, chans), jnp.bfloat16),
            pltpu.VMEM((bands + 4, sectors + 4, STEP * STEP, wide), jnp.bfloat16),
            pltpu.VMEM(taps_out_in.shape, jnp.bfloat16),
            pltpu.VMEM((9, chans, feats), jnp.bfloat16),
            pltpu.VMEM(w_two.shape, jnp.bfloat16),
            pltpu.VMEM((9, max(wide - main, LANES), feats), jnp.bfloat16),
            pltpu.VMEM((bands, sectors, STEP * STEP, feats), jnp.float32),
            pltpu.SemaphoreType.DMA((2 + 2 * halves,)),
            pltpu.SemaphoreType.DMA((2, 3)),
            pltpu.SemaphoreType.DMA((2, 12)),
        ],
        compiler_params=pltpu.CompilerParams(
            collective_id=0, has_side_effects=True, vmem_limit_bytes=62 * 1024 * 1024),
    )(fields, land_sea.T, w_depth, b_depth, taps_out_in, b_one, w_two, b_two)


def solution(mesh):
    return jax.shard_map(
        functools.partial(on_device, mesh.shape["lat"], mesh.shape["lon"]),
        mesh=mesh,
        in_specs=(P("lat", "lon", None), P("lat", "lon"), P(), P(), P(), P(), P(), P()),
        out_specs=P("lat", "lon", None),
        check_vma=False,
    )
```
